256 devices in a mesh: seq: 32 (over y_hi, z, core), ch: 8 (over y_lo, x).
Axes of the slice: x: 4, y: 4 (y_hi: 2, y_lo: 2; y = y_hi * 2 + y_lo), z: 8, core: 2. Of those that a mesh axis runs over, the one named last changes fastest.
Arguments:
- layer_input: bfloat16 [12288, 4096], P('seq'), may hold values from -0.25 to 0.25
- value_proj: bfloat16 [12288, 4096], P('seq', 'ch'), may hold values from -4 to 4
- outer_gate: bfloat16 [12288, 4096], P('seq', 'ch'), may hold values from -1.5 to 1.5
- inner_gate: bfloat16 [12288, 4096], P('seq', 'ch'), may hold values from -4 to 4
- conv_output: bfloat16 [12288, 4096], P('seq', 'ch'), may hold values from -4 to 4
- upstream: bfloat16 [12288, 4096], P('seq'), may hold values from -6 to 6
- in_weight: bfloat16 [4096, 4096], P('seq', 'ch'), may hold values from -0.09375 to 0.09375
- out_weight: bfloat16 [4096, 4096], P('ch', 'seq'), may hold values from -0.09375 to 0.09375
- long_filter: bfloat16 [8, 512, 12288], P('ch', 'seq'), may hold values from -1.5 to 1.5
- short_filter: float32 [8, 512, 3], P('ch', 'seq'), may hold values from -5 to 5
Outputs:
- grad_input: bfloat16 [12288, 4096], P('seq', 'ch')
- grad_outer: bfloat16 [12288, 4096], P('seq', 'ch')
- grad_inner: bfloat16 [12288, 4096], P('seq', 'ch')
- grad_long: float32 [8, 512, 12288], P('ch', 'seq')
- grad_short: float32 [8, 512, 3], P('ch', 'seq')
- grad_inproj: float32 [4096, 4096], P('seq', 'ch')
- grad_outproj: float32 [4096, 4096], P('ch', 'seq')
The draws below stay inside these ranges and needn't reach their ends.
All inputs are finite; a program needn't handle non-finite values.
Results may differ from the reference program's by a relative error of at most 0.02.
Values may be sent and summed in bfloat16 or wider, within the bound.
A program may use at most 128 MiB of HBM per device.

```python
import jax
import jax.numpy as jnp

DI = 4096
DW = 4096
DO = 4096
KS = 3
L = 12288
N_CH = 8


def raised(result, rng, source, target, blocks, factor):
    def block_of(position):
        return (jnp.arange(result.shape[position]) // (result.shape[position] // blocks)).reshape((-1,) + (1,) * (result.ndim - 1 - position))

    near = jax.random.permutation(rng, blocks)[block_of(target)]
    second = (block_of(target) + blocks // 2) % blocks
    return jnp.where((block_of(source) == near) | (block_of(source) == second), factor * result, result)


def block_scale(own_key, dims, pieces, least, top_value):
    def one(dim, parts):
        steps = jax.random.uniform(jax.random.fold_in(jax.random.fold_in(own_key, 6), dim), (parts,), jnp.float32, least / len(pieces), top_value / len(pieces))
        return jnp.repeat(jnp.exp(steps), dims[dim] // parts).reshape((-1,) + (1,) * (len(dims) - dim - 1))

    gain = one(*pieces[0])
    for cut in pieces[1:]:
        gain = gain * one(*cut)
    return gain


def bell_draw(rng, shape, spread, bound, split=(), held_as=jnp.bfloat16):
    level = block_scale(rng, shape, split, -0.22, 0.18) if split else 1.0
    values = jax.random.normal(rng, shape, jnp.float32) * spread * level
    return jnp.minimum(jnp.maximum(values, -bound), bound).astype(held_as)


def gaussian_with(stream_key, shape, spread, limit, split, heavy, dtype=jnp.bfloat16):
    entries = spread * jax.random.normal(stream_key, shape, jnp.float32)
    if split:
        entries = entries * block_scale(stream_key, shape, split, -0.22, 0.18)
    return jnp.clip(raised(entries, jax.random.fold_in(stream_key, 3), *heavy), -limit, limit).astype(dtype)


def setup_inputs(seed: int = 0) -> dict:
    key_list = jax.random.split(jax.random.key(seed), 11)
    layer_input = gaussian_with(key_list[0], (L, DI), (L ** -0.5), 0.25, ((0, 32),), (0, 1, 32, 2.75))
    value_proj = bell_draw(key_list[1], (L, DW), (L ** -0.125), 4.0, ((0, 32), (1, 8)))
    outer_gate = bell_draw(key_list[2], (L, DW), (L ** -0.25), 1.5, ((0, 32), (1, 8)))
    inner_gate = bell_draw(key_list[3], (L, DW), (L ** -0.125), 4.0, ((0, 32), (1, 8)))
    conv_output = bell_draw(key_list[4], (L, DW), (L ** -0.125), 4.0, ((0, 32), (1, 8)))
    upstream = gaussian_with(key_list[5], (L, DO), 1.0, 6.0, ((0, 32),), (0, 1, 32, 2.75))
    in_weight = bell_draw(key_list[6], (DI, DW), DI ** -0.5, 0.09375, ((0, 32), (1, 8)))
    out_weight = bell_draw(key_list[7], (DW, DO), DW ** -0.5, 0.09375, ((0, 8), (1, 32)))
    long_filter = bell_draw(key_list[8], (N_CH, DW // N_CH, L), (L ** -0.25), 1.5, ((0, 8), (1, 32)))
    short_filter = bell_draw(key_list[9], (N_CH, DW // N_CH, KS), 1.0, 5.0, ((0, 8), (1, 32)), jnp.float32)
    return dict(layer_input=layer_input, value_proj=value_proj, outer_gate=outer_gate, inner_gate=inner_gate, conv_output=conv_output, upstream=upstream, in_weight=in_weight, out_weight=out_weight, long_filter=long_filter, short_filter=short_filter)


def correlate(later, earlier):
    total = 2 * later.shape[0]
    spectrum = jnp.fft.rfft(later, n=total, axis=0) * jnp.conj(jnp.fft.rfft(earlier, n=total, axis=0))
    return jnp.fft.irfft(spectrum, n=total, axis=0)[: later.shape[0]]


def reference(layer_input, value_proj, outer_gate, inner_gate, conv_output, upstream, in_weight, out_weight, long_filter, short_filter):
    product = (outer_gate.astype(jnp.float32) * conv_output.astype(jnp.float32)).astype(jnp.bfloat16)
    grad_mix = jnp.dot(upstream, out_weight.T, preferred_element_type=jnp.float32)
    grad_outer = (grad_mix * conv_output.astype(jnp.float32)).astype(jnp.bfloat16)
    grad_conv = (grad_mix * outer_gate.astype(jnp.float32)).astype(jnp.bfloat16)
    grad_outproj = jnp.dot(product.T, upstream, preferred_element_type=jnp.float32)
    taps = short_filter.reshape(DW, KS)
    values = value_proj.astype(jnp.float32)
    past = [jnp.pad(values, ((j, 0), (0, 0)))[:L] for j in range(KS)]
    smooth = taps[:, 0] * past[0]
    for j in range(1, KS):
        smooth = smooth + taps[:, j] * past[j]
    gates = inner_gate.astype(jnp.float32)
    mixed = (gates * smooth).astype(jnp.bfloat16)
    filt = long_filter.reshape(DW, L).T.astype(jnp.float32)
    back = grad_conv.astype(jnp.float32)
    grad_mixed = correlate(back, filt)
    grad_long = correlate(back, mixed.astype(jnp.float32)).T.reshape(N_CH, DW // N_CH, L)
    grad_inner = (grad_mixed * smooth).astype(jnp.bfloat16)
    grad_smooth = grad_mixed * gates
    grad_value = taps[:, 0] * grad_smooth
    for j in range(1, KS):
        grad_value = grad_value + taps[:, j] * jnp.pad(grad_smooth, ((0, j), (0, 0)))[j:]
    grad_value = grad_value.astype(jnp.bfloat16)
    grad_short = jnp.stack([jnp.sum(grad_smooth * past[j], axis=0) for j in range(KS)], axis=1)
    grad_short = grad_short.reshape(N_CH, DW // N_CH, KS)
    grad_input = jnp.dot(grad_value, in_weight.T, preferred_element_type=jnp.float32).astype(jnp.bfloat16)
    grad_inproj = jnp.dot(layer_input.T, grad_value, preferred_element_type=jnp.float32)
    return (grad_input, grad_outer, grad_inner, grad_long, grad_short, grad_inproj, grad_outproj)
```

```python
import math

import ml_dtypes
import numpy as np
import jax
import jax.numpy as jnp
from jax import lax
from jax.experimental import pallas as pl
from jax.experimental.pallas import tpu as pltpu
from jax.sharding import PartitionSpec as P

MESH = pl.DeviceIdType.MESH
F32 = jnp.float32
BF16 = jnp.bfloat16
N_SEQ = 32
ROWS = 384
CHANS = 512
MINE = 16
WIDE = 128
LENGTH = N_SEQ * ROWS
OUTER = LENGTH // WIDE
SIGNS = (1, -1)


def split_table(table):
    high = table.astype(ml_dtypes.bfloat16)
    low = (table - high.astype(np.float64)).astype(ml_dtypes.bfloat16)
    return high, low


def dft_tables():
    order = np.array([3 * s + q for q in range(3) for s in range(N_SEQ)])
    a = np.arange(OUTER)
    b = np.arange(WIDE)
    k1 = np.arange(OUTER)
    k2 = np.arange(WIDE)
    turn = np.pi / (2 * LENGTH)
    outer = 2 * np.pi * np.outer(k1, a) / OUTER + turn * WIDE * a[None, :]
    twist = 2 * np.pi * np.outer(k1, b) / LENGTH + turn * b[None, :]
    inner = 2 * np.pi * np.outer(b, k2) / WIDE
    first = np.concatenate([np.cos(outer), -np.sin(outer)], axis=0)[:, order]
    co, si = np.cos(inner), np.sin(inner)
    second = np.block([[co, -si], [si, co]])
    third = np.block([[co, si], [-si, co]])
    last = np.concatenate([np.cos(outer).T, -np.sin(outer).T], axis=1) / LENGTH
    first_h, first_l = split_table(first)
    second_h, second_l = split_table(second)
    third_h, third_l = split_table(third)
    perm_h, perm_l = split_table(last[order])
    last_h, last_l = split_table(last)
    return (
        np.concatenate([first_h, first_l], axis=0),
        second_h,
        second_l,
        third_h,
        third_l,
        np.stack([perm_h, perm_l, last_h, last_l]),
        np.cos(twist).astype(np.float32),
        np.sin(twist).astype(np.float32),
    )


def remote(src, dst, send, recv, axis, index):
    return pltpu.make_async_remote_copy(
        src_ref=src,
        dst_ref=dst,
        send_sem=send,
        recv_sem=recv,
        device_id={axis: index},
        device_id_type=MESH,
    )


def place():
    s = lax.axis_index("seq")
    return s, s // 16, (s // 2) % 8, s % 2


def at_seq(y, z, c):
    return y * 16 + z * 2 + c


def greet_all(barrier, s):
    def body(i, _):
        pl.semaphore_signal(
            barrier, inc=1, device_id={"seq": (s + i) % N_SEQ}, device_id_type=MESH
        )
        return 0

    lax.fori_loop(1, N_SEQ, body, 0)


def exchange(source_of, target, sends, recvs, s):
    def body(i, _):
        dst = (s + i) % N_SEQ
        remote(source_of(dst), target, sends.at[i], recvs.at[i], "seq", dst).start()
        return 0

    lax.fori_loop(1, N_SEQ, body, 0)


def arrived(landing_of, sends, recvs, s):
    def body(i, _):
        src = (s + N_SEQ - i) % N_SEQ
        here = landing_of(src)
        remote(here, here, sends.at[i], recvs.at[i], "seq", src).wait_recv()
        return 0

    lax.fori_loop(1, N_SEQ, body, 0)


def left(piece, sends, recvs, s):
    def body(i, _):
        remote(piece, piece, sends.at[i], recvs.at[i], "seq", (s + i) % N_SEQ).wait_send()
        return 0

    lax.fori_loop(1, N_SEQ, body, 0)


class Gather:
    sems = [
        pltpu.SemaphoreType.DMA((2, 4, 2)),
        pltpu.SemaphoreType.DMA((2, 4, 2)),
        pltpu.SemaphoreType.DMA((2, 8)),
        pltpu.SemaphoreType.DMA((2, 8)),
        pltpu.SemaphoreType.DMA((2,)),
    ]

    def __init__(self, shard, whole, sems, at):
        self.shard, self.whole, self.at = shard, whole, at
        self.zs, self.zr, self.cs, self.cr, self.ys = sems
        self.started = []

    def slot(self, sub, o, other=False):
        _, y, z, c = self.at
        yy = 1 - y if sub else y
        return at_seq(yy, (z + o + 8) % 8, 1 - c if other else c)

    def go(self, copy):
        copy.start()
        self.started.append(copy)

    def source(self, sub, o):
        if sub == 0 and o == 0:
            return self.shard
        return self.whole.at[self.slot(sub, o)]

    def hop(self, di, d, sub):
        _, y, z, c = self.at
        o = -SIGNS[di] * (d - 1)
        there = at_seq(y, (z + SIGNS[di] + 8) % 8, c)
        self.go(
            remote(
                self.source(sub, o),
                self.whole.at[self.slot(sub, o)],
                self.zs.at[di, d - 1, sub],
                self.zr.at[di, d - 1, sub],
                "seq",
                there,
            )
        )

    def share(self, sub, o):
        _, y, z, c = self.at
        self.go(
            remote(
                self.source(sub, o),
                self.whole.at[self.slot(sub, o)],
                self.cs.at[sub, o % 8],
                self.cr.at[sub, o % 8],
                "seq",
                at_seq(y, z, 1 - c),
            )
        )

    def pair(self):
        _, y, z, c = self.at
        return remote(
            self.shard,
            self.whole.at[self.slot(0, 0)],
            self.ys.at[0],
            self.ys.at[1],
            "seq",
            at_seq(1 - y, z, c),
        )

    @staticmethod
    def travels(di, d, sub):
        return d < 4 or (d == 4 and sub == di)

    def begin(self):
        self.hop(0, 1, 0)
        self.hop(1, 1, 0)
        self.go(self.pair())
        self.share(0, 0)
        self.whole[self.slot(0, 0)] = self.shard[...]

    def steps(self):
        self.pair().wait_recv()
        self.hop(0, 1, 1)
        self.hop(1, 1, 1)
        self.share(1, 0)
        yield
        for d in range(1, 5):
            for sub in range(2):
                for di in range(2):
                    if not self.travels(di, d, sub):
                        continue
                    o = -SIGNS[di] * d
                    here = self.whole.at[self.slot(sub, o)]
                    remote(
                        here,
                        here,
                        self.zs.at[di, d - 1, sub],
                        self.zr.at[di, d - 1, sub],
                        "seq",
                        self.at[0],
                    ).wait_recv()
                    if self.travels(di, d + 1, sub):
                        self.hop(di, d + 1, sub)
                    self.share(sub, o)
                yield

    def ready(self, sub, o):
        _, y, z, c = self.at
        here = self.whole.at[self.slot(sub, o, other=True)]
        remote(
            here, here, self.cs.at[sub, o % 8], self.cr.at[sub, o % 8], "seq", self.at[0]
        ).wait_recv()
        yy = 1 - y if sub else y
        return yy * 8 + (z + o + 8) % 8

    def end(self):
        for copy in self.started:
            copy.wait_send()


class Scatter:
    @staticmethod
    def scratch():
        return [
            pltpu.VMEM((2, 8, CHANS, WIDE), BF16),
            pltpu.VMEM((2, 8, CHANS, WIDE), BF16),
            pltpu.VMEM((2, 8, CHANS, WIDE), BF16),
            pltpu.VMEM((2, 4, 2, CHANS, WIDE), BF16),
            pltpu.VMEM((2, CHANS, WIDE), BF16),
            pltpu.SemaphoreType.DMA((2, 4, 2)),
            pltpu.SemaphoreType.DMA((2, 4, 2)),
            pltpu.SemaphoreType.DMA((2, 8)),
            pltpu.SemaphoreType.DMA((2, 8)),
            pltpu.SemaphoreType.DMA((2,)),
        ]

    def __init__(self, scratch, at):
        self.at = at
        self.own, self.tx, self.rx, self.zrx, self.yrx = scratch[:5]
        self.zs, self.zr, self.cs, self.cr, self.ys = scratch[5:]
        self.started = []

    def go(self, copy):
        copy.start()
        self.started.append(copy)

    def hand(self, sub, o):
        _, y, z, c = self.at
        return remote(
            self.tx.at[sub, o],
            self.rx.at[sub, o],
            self.cs.at[sub, o],
            self.cr.at[sub, o],
            "seq",
            at_seq(y, z, 1 - c),
        )

    def partials(self, left_t, right):
        _, y, z, c = self.at

        def body(i, _):
            o = (4 + (1 - 2 * (i % 2)) * ((i + 1) // 2) + 8) % 8
            for sub in range(2):
                yy = 1 - y if sub else y
                m = yy * 8 + (z + o) % 8
                cols = pl.ds(pl.multiple_of(m * 2 * WIDE, 2 * WIDE), 2 * WIDE)
                part = jnp.dot(left_t[...], right[:, cols], preferred_element_type=F32)
                low = part[:, :WIDE].astype(BF16)
                high = part[:, WIDE:].astype(BF16)
                self.own[sub, o] = jnp.where(c == 0, low, high)
                self.tx[sub, o] = jnp.where(c == 0, high, low)
                self.hand(sub, o).start()
            return 0

        lax.fori_loop(0, 8, body, 0)

    def hop(self, di, d, sub):
        _, y, z, c = self.at
        o = (SIGNS[di] * d) % 8
        there = at_seq(y, (z + SIGNS[di] + 8) % 8, c)
        return remote(
            self.own.at[sub, o],
            self.zrx.at[di, d - 1, sub],
            self.zs.at[di, d - 1, sub],
            self.zr.at[di, d - 1, sub],
            "seq",
            there,
        )

    def pair(self):
        _, y, z, c = self.at
        return remote(
            self.yrx.at[0],
            self.yrx.at[1],
            self.ys.at[0],
            self.ys.at[1],
            "seq",
            at_seq(1 - y, z, c),
        )

    def both(self, sub, o):
        self.hand(sub, o).wait_recv()
        return self.own[sub, o].astype(F32) + self.rx[sub, o].astype(F32)

    def steps(self):
        for d in range(4, 0, -1):
            for sub in range(2):
                for di in range(2):
                    if not Gather.travels(di, d, sub):
                        continue
                    o = (SIGNS[di] * d) % 8
                    total = self.both(sub, o)
                    if Gather.travels(di, d + 1, sub):
                        self.hop(di, d + 1, sub).wait_recv()
                        total = total + self.zrx[di, d, sub].astype(F32)
                    self.own[sub, o] = total.astype(BF16)
                    self.go(self.hop(di, d, sub))
                yield

    def finish(self, out):
        def total(sub):
            value = self.both(sub, 0)
            for di in range(2):
                self.hop(di, 1, sub).wait_recv()
                value = value + self.zrx[di, 0, sub].astype(F32)
            return value

        self.yrx[0] = total(1).astype(BF16)
        self.pair().start()
        out[...] = total(0)
        self.pair().wait_recv()
        out[...] += self.yrx[1].astype(F32)
        self.pair().wait_send()
        for copy in self.started:
            copy.wait_send()

        def body(i, _):
            for sub in range(2):
                self.hand(sub, i).wait_send()
            return 0

        lax.fori_loop(0, 8, body, 0)


def sixteen(index):
    return pl.ds(pl.multiple_of(index * MINE, MINE), MINE)


def front_kernel(
    out_shard, upstream, outer_gate, conv_output, value, gate, taps,
    grad_outer, product_t, conv_rx, mix_rx, padded, all_taps,
    whole, acc, conv_t, mix_t, halo, taps_rx,
    gather_0, gather_1, gather_2, gather_3, gather_4,
    halo_sem, taps_s, taps_r, mix_s, mix_r, conv_s, conv_r,
):
    at = place()
    s, y, z, c = at
    barrier = pltpu.get_barrier_semaphore()
    greet_all(barrier, s)
    pl.semaphore_wait(barrier, N_SEQ - 1)

    ring = Gather(out_shard, whole, (gather_0, gather_1, gather_2, gather_3, gather_4), at)
    ring.begin()
    edge = remote(
        value.at[pl.ds(ROWS - 16, 16)],
        halo,
        halo_sem.at[0],
        halo_sem.at[1],
        "seq",
        (s + 1) % N_SEQ,
    )
    edge.start()
    exchange(lambda d: taps, taps_rx.at[s], taps_s, taps_r, s)
    taps_rx[s] = taps[...]
    step = ring.steps()

    for r in range(0, ROWS, WIDE):
        rows = pl.ds(r, WIDE)
        product = outer_gate[rows, :].astype(F32) * conv_output[rows, :].astype(F32)
        product_t[:, rows] = product.T.astype(BF16)
        padded[pl.ds(8 + r, WIDE), :] = value[rows, :].astype(F32)
    next(step)

    arrived(lambda d: taps_rx.at[d], taps_s, taps_r, s)
    for g in range(4):
        tile = taps_rx[8 * g]
        for i in range(1, 8):
            tile = tile + taps_rx[8 * g + i]
        all_taps[:, pl.ds(g * WIDE, WIDE)] = tile
    edge.wait_recv()
    padded[pl.ds(0, 8), :] = jnp.where(s == 0, 0.0, halo[...].astype(F32)[8:, :])
    next(step)
    for r in range(0, ROWS, WIDE):
        smooth = all_taps[pl.ds(0, 1), :] * padded[pl.ds(8 + r, WIDE), :]
        for j in range(1, 3):
            smooth = smooth + all_taps[pl.ds(j, 1), :] * padded[pl.ds(8 + r - j, WIDE), :]
        mixed = gate[pl.ds(r, WIDE), :].astype(F32) * smooth
        mix_t[:, pl.ds(r, WIDE)] = mixed.T.astype(BF16)
    next(step)
    exchange(lambda d: mix_t.at[sixteen(d)], mix_rx.at[sixteen(s)], mix_s, mix_r, s)
    mix_rx[sixteen(s), :] = mix_t[sixteen(s), :]

    def multiply(sub, o, first=False):
        m = ring.ready(sub, o)
        cols = pl.ds(pl.multiple_of(m * 2 * WIDE, 2 * WIDE), 2 * WIDE)
        shards = jnp.concatenate([whole[2 * m], whole[2 * m + 1]], axis=1)
        part = lax.dot_general(
            upstream[:, cols], shards, (((1,), (1,)), ((), ())), preferred_element_type=F32
        )
        acc[...] = part if first else acc[...] + part

    multiply(0, 0, True)
    multiply(1, 0)
    for d in range(2, 5):
        next(step)
        multiply(0, d - 1)
        multiply(0, 1 - d)
        next(step)
        multiply(1, d - 1)
        multiply(1, 1 - d)
    for _ in step:
        pass
    multiply(0, 4)
    multiply(1, 4)

    for r in range(0, ROWS, WIDE):
        rows = pl.ds(r, WIDE)
        conv = acc[rows, :] * outer_gate[rows, :].astype(F32)
        conv_t[:, rows] = conv.T.astype(BF16)
    exchange(lambda d: conv_t.at[sixteen(d)], conv_rx.at[sixteen(s)], conv_s, conv_r, s)
    conv_rx[sixteen(s), :] = conv_t[sixteen(s), :]
    for r in range(0, ROWS, WIDE):
        rows = pl.ds(r, WIDE)
        grad_outer[rows, :] = (acc[rows, :] * conv_output[rows, :].astype(F32)).astype(BF16)
    ring.end()
    edge.wait_send()
    left(taps, taps_s, taps_r, s)
    left(mix_t.at[sixteen(0)], mix_s, mix_r, s)
    arrived(lambda d: mix_rx.at[sixteen(d)], mix_s, mix_r, s)
    left(conv_t.at[sixteen(0)], conv_s, conv_r, s)
    arrived(lambda d: conv_rx.at[sixteen(d)], conv_s, conv_r, s)


def halves(x):
    high = x.astype(BF16)
    return high, (x - high.astype(F32)).astype(BF16)


def dot(a, b):
    return jnp.dot(a, b, preferred_element_type=F32)


def dot_three(x, table_h, table_l):
    high, low = halves(x)
    return dot(high, table_h) + dot(high, table_l) + dot(low, table_h)


def middle_kernel(
    in_shard, upstream, product_t, conv_cols, mix_cols, filters,
    first, second_h, second_l, third_h, third_l, last, cos_t, sin_t,
    grad_mixed, grad_long, grad_outproj, whole,
    conv_f, mix_f, out_f,
    gather_0, gather_1, gather_2, gather_3, gather_4,
    *scatter,
):
    at = place()
    s, y, z, c = at
    barrier = pltpu.get_barrier_semaphore()
    for there in (
        at_seq(y, (z + 1) % 8, c),
        at_seq(y, (z + 7) % 8, c),
        at_seq(1 - y, z, c),
        at_seq(y, z, 1 - c),
    ):
        pl.semaphore_signal(barrier, inc=1, device_id={"seq": there}, device_id_type=MESH)
    pl.semaphore_wait(barrier, 4)

    ring = Gather(in_shard, whole, (gather_0, gather_1, gather_2, gather_3, gather_4), at)
    total = Scatter(scatter, at)
    ring.begin()
    total.partials(product_t, upstream)
    gather_step = ring.steps()
    scatter_step = total.steps()
    for q in range(3):
        conv_f[q] = conv_cols[:, q * WIDE : (q + 1) * WIDE].astype(F32)
        mix_f[q] = mix_cols[:, q * WIDE : (q + 1) * WIDE].astype(F32)

    def channel(i, _):
        def read(ref):
            return jnp.concatenate(
                [ref[q, pl.ds(i, N_SEQ, stride=MINE), :] for q in range(3)], axis=0
            ).astype(BF16)

        signals = jnp.concatenate([read(conv_f), filters[i], read(mix_f)], axis=1)
        both = dot(first[...], signals)
        both = both[: 2 * OUTER] + both[2 * OUTER :]
        cos, sin = cos_t[...], sin_t[...]
        rows = []
        for n in range(3):
            re = both[:OUTER, n * WIDE : (n + 1) * WIDE]
            im = both[OUTER:, n * WIDE : (n + 1) * WIDE]
            rows.append(jnp.concatenate([re * cos + im * sin, im * cos - re * sin], axis=1))
        spec = dot_three(jnp.concatenate(rows, axis=0), second_h[...], second_l[...])
        g_re, g_im = spec[:OUTER, :WIDE], spec[:OUTER, WIDE:]
        rows = []
        for n in (1, 2):
            re = spec[n * OUTER : (n + 1) * OUTER, :WIDE]
            im = spec[n * OUTER : (n + 1) * OUTER, WIDE:]
            rows.append(jnp.concatenate([g_re * re + g_im * im, g_im * re - g_re * im], axis=1))
        mid = dot_three(jnp.concatenate(rows, axis=0), third_h[...], third_l[...])
        for n in range(2):
            re = mid[n * OUTER : (n + 1) * OUTER, :WIDE]
            im = mid[n * OUTER : (n + 1) * OUTER, WIDE:]
            turned = jnp.concatenate([re * cos - im * sin, im * cos + re * sin], axis=0)
            high, low = halves(turned)
            result = dot(last[2 * n], high) + dot(last[2 * n + 1], high) + dot(last[2 * n], low)
            if n == 0:
                for q in range(3):
                    out_f[q, pl.ds(i, N_SEQ, stride=MINE), :] = result[
                        q * N_SEQ : (q + 1) * N_SEQ
                    ]
            else:
                grad_long[i] = result
        return 0

    for n in range(8):
        next(gather_step, None)
        next(scatter_step, None)
        lax.fori_loop(2 * n, 2 * n + 2, channel, 0)
    for q in range(3):
        grad_mixed[:, q * WIDE : (q + 1) * WIDE] = out_f[q].astype(BF16)
    for _ in range(16):
        next(gather_step, None)
        next(scatter_step, None)
    total.finish(grad_outproj)
    for sub in range(2):
        for o in range(-3, 5):
            ring.ready(sub, o)
    ring.end()


def back_kernel(
    mixed_cols, padded, all_taps, gate, layer_input, weights,
    grad_inner, grad_input, grad_inproj, grad_short,
    mixed_rx, grads, halo, value, value_t, blocks, short_tx, short_rx, acc,
    halo_sem, mix_s, mix_r, short_s, short_r, x_s, x_r, p_s,
    *scatter,
):
    at = place()
    s, y, z, c = at
    ch = lax.axis_index("ch")
    x, low = ch % 4, ch // 4
    barrier = pltpu.get_barrier_semaphore()
    greet_all(barrier, s)
    for there in (low * 4 + (x + 1) % 4, low * 4 + (x + 3) % 4, (1 - low) * 4 + x):
        pl.semaphore_signal(barrier, inc=1, device_id={"ch": there}, device_id_type=MESH)
    pl.semaphore_wait(barrier, N_SEQ - 1 + 3)

    exchange(lambda d: mixed_cols.at[sixteen(d)], mixed_rx.at[sixteen(s)], mix_s, mix_r, s)
    mixed_rx[sixteen(s), :] = mixed_cols[sixteen(s), :]
    arrived(lambda d: mixed_rx.at[sixteen(d)], mix_s, mix_r, s)

    edge = remote(
        grads.at[pl.ds(0, 8)],
        halo,
        halo_sem.at[0],
        halo_sem.at[1],
        "seq",
        (s + N_SEQ - 1) % N_SEQ,
    )
    for r in range(0, ROWS, WIDE):
        rows = pl.ds(r, WIDE)
        mixed = mixed_rx[:, rows].astype(F32).T
        grads[rows, :] = mixed * gate[rows, :].astype(F32)
        if r == 0:
            edge.start()
        smooth = all_taps[pl.ds(0, 1), :] * padded[pl.ds(8 + r, WIDE), :]
        for j in range(1, 3):
            smooth = smooth + all_taps[pl.ds(j, 1), :] * padded[pl.ds(8 + r - j, WIDE), :]
        grad_inner[rows, :] = (mixed * smooth).astype(BF16)
    edge.wait_recv()
    grads[pl.ds(ROWS, 8), :] = jnp.where(s == N_SEQ - 1, 0.0, halo[...])
    for r in range(0, ROWS, WIDE):
        rows = pl.ds(r, WIDE)
        out = all_taps[pl.ds(0, 1), :] * grads[rows, :]
        for j in range(1, 3):
            out = out + all_taps[pl.ds(j, 1), :] * grads[pl.ds(r + j, WIDE), :]
        value[rows, :] = out.astype(BF16)
        value_t[:, rows] = out.T.astype(BF16)

    def block(sub, o):
        return (1 - low if sub else low) * 4 + (x + o + 4) % 4

    def x_source(sub, o):
        return value if (sub, o) == (0, 0) else blocks.at[block(sub, o)]

    def x_hop(di, d, sub):
        o = -SIGNS[di] * (d - 1)
        return remote(
            x_source(sub, o),
            blocks.at[block(sub, o)],
            x_s.at[di, d - 1, sub],
            x_r.at[di, d - 1, sub],
            "ch",
            low * 4 + (x + SIGNS[di] + 4) % 4,
        )

    def x_wait(di, d, sub):
        here = blocks.at[block(sub, -SIGNS[di] * d)]
        remote(
            here, here, x_s.at[di, d - 1, sub], x_r.at[di, d - 1, sub], "ch", ch
        ).wait_recv()

    partner = remote(
        value, blocks.at[block(0, 0)], p_s.at[0], p_s.at[1], "ch", (1 - low) * 4 + x
    )
    hops = [x_hop(0, 1, 0), x_hop(1, 1, 0)]
    hops[0].start()
    hops[1].start()
    partner.start()
    blocks[block(0, 0)] = value[...]

    total = Scatter(scatter, at)
    total.partials(value_t, layer_input)
    step = total.steps()
    next(step)
    next(step)

    sums = []
    for j in range(3):
        part = jnp.zeros((1, CHANS), F32)
        for r in range(0, ROWS, WIDE):
            part = part + jnp.sum(
                grads[pl.ds(r, WIDE), :] * padded[pl.ds(8 + r - j, WIDE), :], axis=0, keepdims=True
            )
        sums.append(part)
    short_tx[...] = jnp.concatenate(sums + [jnp.zeros((5, CHANS), F32)], axis=0)

    def lanes(d):
        return short_tx.at[:, pl.ds(pl.multiple_of(d // 8 * WIDE, WIDE), WIDE)]

    exchange(lanes, short_rx.at[s], short_s, short_r, s)
    short_rx[s] = short_tx[:, pl.ds(pl.multiple_of(s // 8 * WIDE, WIDE), WIDE)]

    def multiply(n, first=False):
        w = jnp.concatenate([weights[4 * n + i] for i in range(4)], axis=0)
        part = lax.dot_general(
            blocks[n], w, (((1,), (1,)), ((), ())), preferred_element_type=F32
        )
        acc[...] = part if first else acc[...] + part

    multiply(ch, True)
    next(step)
    partner.wait_recv()
    for di in range(2):
        hop = x_hop(di, 1, 1)
        hop.start()
        hops.append(hop)
    multiply(block(1, 0))
    next(step)
    x_wait(0, 1, 0)
    hop = x_hop(0, 2, 0)
    hop.start()
    hops.append(hop)
    multiply(block(0, -1))
    next(step)
    x_wait(1, 1, 0)
    multiply(block(0, 1))
    next(step)
    x_wait(1, 1, 1)
    hop = x_hop(1, 2, 1)
    hop.start()
    hops.append(hop)
    multiply(block(1, 1))
    for _ in step:
        pass
    x_wait(0, 1, 1)
    multiply(block(1, -1))
    total.finish(grad_inproj)
    arrived(lambda d: short_rx.at[d], short_s, short_r, s)
    tile = short_rx[0]
    for i in range(1, N_SEQ):
        tile = tile + short_rx[i]
    grad_short[...] = tile
    x_wait(0, 2, 0)
    multiply(block(0, 2))
    x_wait(1, 2, 1)
    multiply(block(1, 2))
    grad_input[...] = acc[...].astype(BF16)
    for hop in hops:
        hop.wait_send()
    partner.wait_send()
    edge.wait_send()
    left(mixed_cols.at[sixteen(0)], mix_s, mix_r, s)
    left(short_rx.at[0], short_s, short_r, s)


def call(kernel, outs, scratch, collective_id, args, flops):
    vmem = pl.BlockSpec(memory_space=pltpu.VMEM)
    return pl.pallas_call(
        kernel,
        out_shape=[jax.ShapeDtypeStruct(shape, dtype) for shape, dtype in outs],
        in_specs=[vmem] * len(args),
        out_specs=[vmem] * len(outs),
        scratch_shapes=scratch,
        compiler_params=pltpu.CompilerParams(
            collective_id=collective_id, has_side_effects=True, vmem_limit_bytes=50 * 2**20
        ),
        cost_estimate=pl.CostEstimate(
            flops=flops, bytes_accessed=20 * 2**20, transcendentals=0
        ),
    )(*args)


def shards(
    layer_input, value_proj, outer_gate, inner_gate, conv_output,
    upstream, in_weight, out_weight, long_filter, short_filter,
):
    s = lax.axis_index("seq")
    dma = pltpu.SemaphoreType.DMA
    peers = dma((N_SEQ,))
    turned = [
        ((4 * to + i) * 8 + ch, (4 * ch + i) * 8 + to)
        for to in range(8)
        for ch in range(8)
        for i in range(4)
    ]
    in_piece = lax.ppermute(in_weight, ("seq", "ch"), turned)
    lane = (s % 8) * MINE
    taps = lax.dynamic_update_slice(
        jnp.zeros((8, WIDE), F32), short_filter[0].T, (jnp.int32(0), lane.astype(jnp.int32))
    )
    filters = long_filter[0].reshape(MINE, N_SEQ, 3, WIDE)
    filters = filters.transpose(0, 2, 1, 3).reshape(MINE, OUTER, WIDE)

    grad_outer, product_t, conv_cols, mix_cols, padded, all_taps = call(
        front_kernel,
        [
            ((ROWS, CHANS), BF16),
            ((CHANS, ROWS), BF16),
            ((CHANS, ROWS), BF16),
            ((CHANS, ROWS), BF16),
            ((ROWS + 8, CHANS), F32),
            ((8, CHANS), F32),
        ],
        [
            pltpu.VMEM((N_SEQ, CHANS, WIDE), BF16),
            pltpu.VMEM((ROWS, CHANS), F32),
            pltpu.VMEM((CHANS, ROWS), BF16),
            pltpu.VMEM((CHANS, ROWS), BF16),
            pltpu.VMEM((16, CHANS), BF16),
            pltpu.VMEM((N_SEQ, 8, WIDE), F32),
            *Gather.sems,
            dma((2,)), peers, peers, peers, peers, peers, peers,
        ],
        0,
        (out_weight, upstream, outer_gate, conv_output, value_proj, inner_gate, taps),
        2 * 10**9,
    )
    tables = [jnp.asarray(t) for t in dft_tables()]
    grad_mixed, grad_long, grad_outproj, weights = call(
        middle_kernel,
        [
            ((CHANS, ROWS), BF16),
            ((MINE, OUTER, WIDE), F32),
            ((CHANS, WIDE), F32),
            ((N_SEQ, WIDE, CHANS), BF16),
        ],
        [
            pltpu.VMEM((3, CHANS, WIDE), F32),
            pltpu.VMEM((3, CHANS, WIDE), F32),
            pltpu.VMEM((3, CHANS, WIDE), F32),
            *Gather.sems,
            *Scatter.scratch(),
        ],
        1,
        (in_piece, upstream, product_t, conv_cols, mix_cols, filters, *tables),
        6 * 10**9,
    )
    grad_inner, grad_input, grad_inproj, grad_short = call(
        back_kernel,
        [
            ((ROWS, CHANS), BF16),
            ((ROWS, CHANS), BF16),
            ((CHANS, WIDE), F32),
            ((8, WIDE), F32),
        ],
        [
            pltpu.VMEM((CHANS, ROWS), BF16),
            pltpu.VMEM((ROWS + 8, CHANS), F32),
            pltpu.VMEM((8, CHANS), F32),
            pltpu.VMEM((ROWS, CHANS), BF16),
            pltpu.VMEM((CHANS, ROWS), BF16),
            pltpu.VMEM((8, ROWS, CHANS), BF16),
            pltpu.VMEM((8, CHANS), F32),
            pltpu.VMEM((N_SEQ, 8, WIDE), F32),
            pltpu.VMEM((ROWS, CHANS), F32),
            dma((2,)), peers, peers, peers, peers, dma((2, 2, 2)), dma((2, 2, 2)), dma((2,)),
            *Scatter.scratch(),
        ],
        2,
        (grad_mixed, padded, all_taps, inner_gate, layer_input, weights),
        4 * 10**9,
    )
    grad_taps = lax.dynamic_slice(
        grad_short, (jnp.int32(0), lane.astype(jnp.int32)), (3, MINE)
    ).T
    return (
        grad_input,
        grad_outer,
        grad_inner,
        grad_long.reshape(1, MINE, LENGTH),
        grad_taps[None],
        grad_inproj.T,
        grad_outproj,
    )


def solution(mesh):
    in_specs = (
        P("seq", None),
        P("seq", "ch"),
        P("seq", "ch"),
        P("seq", "ch"),
        P("seq", "ch"),
        P("seq", None),
        P("seq", "ch"),
        P("ch", "seq"),
        P("ch", "seq", None),
        P("ch", "seq", None),
    )
    out_specs = (
        P("seq", "ch"),
        P("seq", "ch"),
        P("seq", "ch"),
        P("ch", "seq", None),
        P("ch", "seq", None),
        P("seq", "ch"),
        P("ch", "seq"),
    )
    return jax.shard_map(shards, mesh=mesh, in_specs=in_specs, out_specs=out_specs, check_vma=False)
```

```python
import math

import ml_dtypes
import numpy as np
import jax
import jax.numpy as jnp
from jax import lax
from jax.experimental import pallas as pl
from jax.experimental.pallas import tpu as pltpu
from jax.sharding import PartitionSpec as P

MESH = pl.DeviceIdType.MESH
F32 = jnp.float32
BF16 = jnp.bfloat16
N_SEQ = 32
ROWS = 384
CHANS = 512
MINE = 16
WIDE = 128
DEEP = 4096
LENGTH = N_SEQ * ROWS
OUTER = LENGTH // WIDE
SIGNS = (1, -1)


def split_table(table):
    high = table.astype(ml_dtypes.bfloat16)
    low = (table - high.astype(np.float64)).astype(ml_dtypes.bfloat16)
    return high, low


def dft_tables():
    a = np.arange(OUTER)
    b = np.arange(WIDE)
    k1 = np.arange(OUTER)
    k2 = np.arange(WIDE)
    turn = np.pi / (2 * LENGTH)
    outer = 2 * np.pi * np.outer(k1, a) / OUTER + turn * WIDE * a[None, :]
    twist = 2 * np.pi * np.outer(k1, b) / LENGTH + turn * b[None, :]
    inner = 2 * np.pi * np.outer(b, k2) / WIDE
    first = np.concatenate([np.cos(outer), -np.sin(outer)], axis=0)
    co, si = np.cos(inner), np.sin(inner)
    second = np.block([[co, -si], [si, co]])
    third = np.block([[co, si], [-si, co]])
    last = np.concatenate([np.cos(outer).T, -np.sin(outer).T], axis=1) / LENGTH
    first_h, first_l = split_table(first)
    second_h, second_l = split_table(second)
    third_h, third_l = split_table(third)
    last_h, last_l = split_table(last)
    return (
        np.concatenate([first_h, first_l], axis=0),
        second_h,
        second_l,
        third_h,
        third_l,
        np.stack([last_h, last_l]),
        np.cos(twist).astype(np.float32),
        np.sin(twist).astype(np.float32),
    )


def remote_to(src, dst, send, recv, device):
    return pltpu.make_async_remote_copy(
        src_ref=src,
        dst_ref=dst,
        send_sem=send,
        recv_sem=recv,
        device_id=device,
        device_id_type=MESH,
    )


def remote(src, dst, send, recv, axis, index):
    return remote_to(src, dst, send, recv, {axis: index})


def place():
    s = lax.axis_index("seq")
    return s, s // 16, (s // 2) % 8, s % 2


def at_seq(y, z, c):
    return y * 16 + z * 2 + c


def greet_all(barrier, s):
    def body(i, _):
        pl.semaphore_signal(
            barrier, inc=1, device_id={"seq": (s + i) % N_SEQ}, device_id_type=MESH
        )
        return 0

    lax.fori_loop(1, N_SEQ, body, 0)


def exchange(source_of, target, sends, recvs, s):
    def body(i, _):
        dst = (s + i) % N_SEQ
        remote(source_of(dst), target, sends.at[i], recvs.at[i], "seq", dst).start()
        return 0

    lax.fori_loop(1, N_SEQ, body, 0)


def arrived(landing_of, sends, recvs, s):
    def body(i, _):
        src = (s + N_SEQ - i) % N_SEQ
        here = landing_of(src)
        remote(here, here, sends.at[i], recvs.at[i], "seq", src).wait_recv()
        return 0

    lax.fori_loop(1, N_SEQ, body, 0)


def left(piece, sends, recvs, s):
    def body(i, _):
        remote(piece, piece, sends.at[i], recvs.at[i], "seq", (s + i) % N_SEQ).wait_send()
        return 0

    lax.fori_loop(1, N_SEQ, body, 0)


class Gather:
    sems = [
        pltpu.SemaphoreType.DMA((2, 4, 2)),
        pltpu.SemaphoreType.DMA((2, 4, 2)),
        pltpu.SemaphoreType.DMA((2, 8)),
        pltpu.SemaphoreType.DMA((2, 8)),
        pltpu.SemaphoreType.DMA((3,)),
    ]

    def __init__(self, shard, whole, sems, at):
        self.shard, self.whole, self.at = shard, whole, at
        self.zs, self.zr, self.cs, self.cr, self.ys = sems
        self.started = []

    def slot(self, sub, o, other=False):
        _, y, z, c = self.at
        yy = 1 - y if sub else y
        return at_seq(yy, (z + o + 8) % 8, 1 - c if other else c)

    def go(self, copy):
        copy.start()
        self.started.append(copy)

    def source(self, sub, o):
        if sub == 0 and o == 0:
            return self.shard
        return self.whole.at[self.slot(sub, o)]

    def hop(self, di, d, sub):
        _, y, z, c = self.at
        o = -SIGNS[di] * (d - 1)
        there = at_seq(y, (z + SIGNS[di] + 8) % 8, c)
        self.go(
            remote(
                self.source(sub, o),
                self.whole.at[self.slot(sub, o)],
                self.zs.at[di, d - 1, sub],
                self.zr.at[di, d - 1, sub],
                "seq",
                there,
            )
        )

    def share(self, sub, o):
        _, y, z, c = self.at
        self.go(
            remote(
                self.source(sub, o),
                self.whole.at[self.slot(sub, o)],
                self.cs.at[sub, o % 8],
                self.cr.at[sub, o % 8],
                "seq",
                at_seq(y, z, 1 - c),
            )
        )

    def pair(self):
        _, y, z, c = self.at
        return remote(
            self.shard,
            self.whole.at[self.slot(0, 0)],
            self.ys.at[0],
            self.ys.at[1],
            "seq",
            at_seq(1 - y, z, c),
        )

    @staticmethod
    def travels(di, d, sub):
        return d < 4 or (d == 4 and sub == di)

    def begin(self):
        self.hop(0, 1, 0)
        self.hop(1, 1, 0)
        self.go(self.pair())
        self.share(0, 0)
        self.keep = pltpu.make_async_copy(
            self.shard, self.whole.at[self.slot(0, 0)], self.ys.at[2]
        )
        self.keep.start()

    def steps(self):
        self.pair().wait_recv()
        self.hop(0, 1, 1)
        self.hop(1, 1, 1)
        self.share(1, 0)
        yield
        for d in range(1, 5):
            for sub in range(2):
                for di in range(2):
                    if not self.travels(di, d, sub):
                        continue
                    o = -SIGNS[di] * d
                    here = self.whole.at[self.slot(sub, o)]
                    remote(
                        here,
                        here,
                        self.zs.at[di, d - 1, sub],
                        self.zr.at[di, d - 1, sub],
                        "seq",
                        self.at[0],
                    ).wait_recv()
                    if self.travels(di, d + 1, sub):
                        self.hop(di, d + 1, sub)
                    self.share(sub, o)
                yield

    def ready(self, sub, o):
        _, y, z, c = self.at
        if (sub, o) == (0, 0):
            self.keep.wait()
        here = self.whole.at[self.slot(sub, o, other=True)]
        remote(
            here, here, self.cs.at[sub, o % 8], self.cr.at[sub, o % 8], "seq", self.at[0]
        ).wait_recv()
        yy = 1 - y if sub else y
        return yy * 8 + (z + o + 8) % 8

    def end(self):
        for copy in self.started:
            copy.wait_send()


class Scatter:
    @staticmethod
    def scratch():
        return [
            pltpu.VMEM((2, 8, CHANS, WIDE), BF16),
            pltpu.VMEM((2, 8, CHANS, WIDE), BF16),
            pltpu.VMEM((2, 8, CHANS, WIDE), BF16),
            pltpu.VMEM((2, 4, 2, CHANS, WIDE), BF16),
            pltpu.VMEM((2, CHANS, WIDE), BF16),
            pltpu.SemaphoreType.DMA((2, 4, 2)),
            pltpu.SemaphoreType.DMA((2, 4, 2)),
            pltpu.SemaphoreType.DMA((2, 8)),
            pltpu.SemaphoreType.DMA((2, 8)),
            pltpu.SemaphoreType.DMA((2,)),
        ]

    def __init__(self, scratch, at):
        self.at = at
        self.own, self.tx, self.rx, self.zrx, self.yrx = scratch[:5]
        self.zs, self.zr, self.cs, self.cr, self.ys = scratch[5:]
        self.started = []

    def go(self, copy):
        copy.start()
        self.started.append(copy)

    def hand(self, sub, o):
        _, y, z, c = self.at
        return remote(
            self.tx.at[sub, o],
            self.rx.at[sub, o],
            self.cs.at[sub, o],
            self.cr.at[sub, o],
            "seq",
            at_seq(y, z, 1 - c),
        )

    def partials(self, left_t, right, first=0, last=8):
        _, y, z, c = self.at

        def body(i, _):
            o = (4 + (1 - 2 * (i % 2)) * ((i + 1) // 2) + 8) % 8
            columns = []
            for sub in range(2):
                m = (1 - y if sub else y) * 8 + (z + o) % 8
                columns.append(right[:, pl.ds(pl.multiple_of(m * 2 * WIDE, 2 * WIDE), 2 * WIDE)])
            both = jnp.dot(
                left_t[...], jnp.concatenate(columns, axis=1), preferred_element_type=F32
            )
            for sub in range(2):
                low = both[:, 2 * sub * WIDE : (2 * sub + 1) * WIDE].astype(BF16)
                high = both[:, (2 * sub + 1) * WIDE : (2 * sub + 2) * WIDE].astype(BF16)
                self.tx[sub, o] = jnp.where(c == 0, high, low)
                self.hand(sub, o).start()
                self.own[sub, o] = jnp.where(c == 0, low, high)
            return 0

        lax.fori_loop(first, last, body, 0)

    def hop(self, di, d, sub):
        _, y, z, c = self.at
        o = (SIGNS[di] * d) % 8
        there = at_seq(y, (z + SIGNS[di] + 8) % 8, c)
        return remote(
            self.own.at[sub, o],
            self.zrx.at[di, d - 1, sub],
            self.zs.at[di, d - 1, sub],
            self.zr.at[di, d - 1, sub],
            "seq",
            there,
        )

    def pair(self):
        _, y, z, c = self.at
        return remote(
            self.yrx.at[0],
            self.yrx.at[1],
            self.ys.at[0],
            self.ys.at[1],
            "seq",
            at_seq(1 - y, z, c),
        )

    def both(self, sub, o):
        self.hand(sub, o).wait_recv()
        return self.own[sub, o].astype(F32) + self.rx[sub, o].astype(F32)

    def steps(self):
        for d in range(4, 0, -1):
            for sub in range(2):
                for di in range(2):
                    if not Gather.travels(di, d, sub):
                        continue
                    o = (SIGNS[di] * d) % 8
                    total = self.both(sub, o)
                    if Gather.travels(di, d + 1, sub):
                        self.hop(di, d + 1, sub).wait_recv()
                        total = total + self.zrx[di, d, sub].astype(F32)
                    self.own[sub, o] = total.astype(BF16)
                    self.go(self.hop(di, d, sub))
                yield

    def finish(self, out):
        def total(sub):
            value = self.both(sub, 0)
            for di in range(2):
                self.hop(di, 1, sub).wait_recv()
                value = value + self.zrx[di, 0, sub].astype(F32)
            return value

        self.yrx[0] = total(1).astype(BF16)
        self.pair().start()
        out[...] = total(0)
        self.pair().wait_recv()
        out[...] += self.yrx[1].astype(F32)
        self.pair().wait_send()
        for copy in self.started:
            copy.wait_send()

        def body(i, _):
            for sub in range(2):
                self.hand(sub, i).wait_send()
            return 0

        lax.fori_loop(0, 8, body, 0)


def sixteen(index):
    return pl.ds(pl.multiple_of(index * MINE, MINE), MINE)


def halves(x):
    high = x.astype(BF16)
    return high, (x - high.astype(F32)).astype(BF16)


def dot(a, b):
    return jnp.dot(a, b, preferred_element_type=F32)


def dot_three(x, table_h, table_l):
    high, low = halves(x)
    return dot(high, table_h[...]) + dot(high, table_l[...]) + dot(low, table_h[...])


class Spectra:
    def __init__(self, tables):
        (
            self.first,
            self.second_h,
            self.second_l,
            self.third_h,
            self.third_l,
            self.last,
            self.cos_t,
            self.sin_t,
        ) = tables

    def forward(self, source, i):
        signals = jnp.concatenate(
            [source[pl.ds(2 * i + n, OUTER, stride=MINE), :] for n in range(2)], axis=1
        ).astype(BF16)
        both = dot(self.first[...], signals)
        both = both[: 2 * OUTER] + both[2 * OUTER :]
        cos, sin = self.cos_t[...], self.sin_t[...]
        rows = []
        for n in range(2):
            re = both[:OUTER, n * WIDE : (n + 1) * WIDE]
            im = both[OUTER:, n * WIDE : (n + 1) * WIDE]
            rows.append(jnp.concatenate([re * cos + im * sin, im * cos - re * sin], axis=1))
        return dot_three(jnp.concatenate(rows, axis=0), self.second_h, self.second_l)

    def inverse(self, later, earlier, target, i):
        a, b = later[:, :WIDE], later[:, WIDE:]
        c, d = earlier[:, :WIDE], earlier[:, WIDE:]
        spec = jnp.concatenate([a * c + b * d, b * c - a * d], axis=1)
        mid = dot_three(spec, self.third_h, self.third_l)
        cos, sin = self.cos_t[...], self.sin_t[...]
        turned = []
        for n in range(2):
            re = mid[n * OUTER : (n + 1) * OUTER, :WIDE]
            im = mid[n * OUTER : (n + 1) * OUTER, WIDE:]
            turned.append(jnp.concatenate([re * cos - im * sin, im * cos + re * sin], axis=0))
        high, low = halves(jnp.concatenate(turned, axis=1))
        result = dot(self.last[0], high) + dot(self.last[1], high) + dot(self.last[0], low)
        for n in range(2):
            target[pl.ds(2 * i + n, OUTER, stride=MINE), :] = result[
                :, n * WIDE : (n + 1) * WIDE
            ]


def spread(cols, target):
    def body(s, _):
        for q in range(3):
            target[sixteen(3 * s + q), :] = cols[sixteen(s), q * WIDE : (q + 1) * WIDE].astype(F32)
        return 0

    lax.fori_loop(0, N_SEQ, body, 0)


def lanes_at(index):
    return pl.ds(pl.multiple_of(index * WIDE, WIDE), WIDE)


def whole_kernel(*refs):
    (
        layer_hbm, value_hbm, outer_hbm, gate_hbm, conv_hbm, up_hbm, in_shard, out_shard, filter_hbm, taps,
        *table_hbm,
    ) = refs[:18]
    (
        grad_input, grad_outer, grad_inner, grad_long, grad_short, grad_inproj, grad_outproj,
    ) = refs[18:25]
    (
        layer_input, value_in, outer_gate, gate, conv_output, upstream, filters, *tables,
    ) = refs[25:40]
    (
        whole_out, whole_in, acc, product_t, conv_t, mix_t, conv_rx, mix_rx, mixed_cols, mixed_rx,
        value, value_t, x_own, x_rx, y_io, padded, all_taps, halo, taps_rx, grads, halo_back, short_tx, short_rx,
        conv_f, other_f, out_f, spec_g, spec_h, inproj_t,
        load_sem, halo_sem, taps_s, taps_r, mix_s, mix_r, conv_s, conv_r,
        back_s, back_r, short_s, short_r, x_s, x_r, p_s,
    ) = refs[40:84]
    rest = refs[84:]
    sems_out, sems_in = rest[:5], rest[5:10]
    scatter_out, scatter_in = rest[10:20], rest[20:30]

    at = place()
    s, y, z, c = at
    ch = lax.axis_index("ch")
    x, low = ch % 4, ch // 4

    barrier = pltpu.get_barrier_semaphore()
    greet_all(barrier, s)
    for there in (low * 4 + (x + 1) % 4, low * 4 + (x + 3) % 4, (1 - low) * 4 + x):
        pl.semaphore_signal(barrier, inc=1, device_id={"ch": there}, device_id_type=MESH)

    sources = [outer_hbm, conv_hbm, value_hbm, gate_hbm, up_hbm, filter_hbm, layer_hbm, *table_hbm]
    targets = [outer_gate, conv_output, value_in, gate, upstream, filters, layer_input, *tables]
    loads = {}
    for n, (src, dst) in enumerate(zip(sources, targets)):
        copy = pltpu.make_async_copy(src, dst, load_sem.at[n])
        copy.start()
        loads[n] = copy

    def loaded(*which):
        for n in which:
            loads[n].wait()

    pl.semaphore_wait(barrier, N_SEQ - 1 + 3)

    ring = Gather(out_shard, whole_out, sems_out, at)
    ring.begin()
    edge = remote(
        value_hbm.at[pl.ds(ROWS - 16, 16)],
        halo,
        halo_sem.at[0],
        halo_sem.at[1],
        "seq",
        (s + 1) % N_SEQ,
    )
    edge.start()
    exchange(lambda d: taps, taps_rx.at[s], taps_s, taps_r, s)
    taps_own = pltpu.make_async_copy(taps, taps_rx.at[s], halo_sem.at[4])
    taps_own.start()
    step = ring.steps()
    loaded(0, 1)
    for r in range(0, ROWS, WIDE):
        rows = pl.ds(r, WIDE)
        product = outer_gate[rows, :].astype(F32) * conv_output[rows, :].astype(F32)
        product_t[:, rows] = product.T.astype(BF16)
    next(step)

    loaded(2, 3)
    for r in range(0, ROWS, WIDE):
        padded[pl.ds(8 + r, WIDE), :] = value_in[pl.ds(r, WIDE), :].astype(F32)
    arrived(lambda d: taps_rx.at[d], taps_s, taps_r, s)
    taps_own.wait()
    for g in range(4):
        tile = taps_rx[8 * g]
        for i in range(1, 8):
            tile = tile + taps_rx[8 * g + i]
        all_taps[:, pl.ds(g * WIDE, WIDE)] = tile
    edge.wait_recv()
    padded[pl.ds(0, 8), :] = jnp.where(s == 0, 0.0, halo[...].astype(F32)[8:, :])
    next(step)

    def smooth_rows(r):
        smooth = all_taps[pl.ds(0, 1), :] * padded[pl.ds(8 + r, WIDE), :]
        for j in range(1, 3):
            smooth = smooth + all_taps[pl.ds(j, 1), :] * padded[pl.ds(8 + r - j, WIDE), :]
        return smooth

    for r in range(0, ROWS, WIDE):
        mixed = gate[pl.ds(r, WIDE), :].astype(F32) * smooth_rows(r)
        mix_t[:, pl.ds(r, WIDE)] = mixed.T.astype(BF16)
    outs = Scatter(scatter_out, at)
    next(step)

    def multiply(sub, o, first=False):
        m = ring.ready(sub, o)
        cols = pl.ds(pl.multiple_of(m * 2 * WIDE, 2 * WIDE), 2 * WIDE)
        shards = jnp.concatenate([whole_out[2 * m], whole_out[2 * m + 1]], axis=1)
        part = lax.dot_general(
            upstream[:, cols], shards, (((1,), (1,)), ((), ())), preferred_element_type=F32
        )
        acc[...] = part if first else acc[...] + part

    loaded(4)
    multiply(0, 0, True)
    multiply(1, 0)
    outs.partials(product_t, upstream, 0, 1)
    for d in range(2, 5):
        next(step)
        multiply(0, d - 1)
        multiply(0, 1 - d)
        outs.partials(product_t, upstream, 2 * d - 3, 2 * d - 2)
        next(step)
        multiply(1, d - 1)
        multiply(1, 1 - d)
        if d < 4:
            outs.partials(product_t, upstream, 2 * d - 2, 2 * d - 1)
    for _ in step:
        pass
    multiply(0, 4)
    multiply(1, 4)

    for r in range(0, ROWS, WIDE):
        rows = pl.ds(r, WIDE)
        conv = acc[rows, :] * outer_gate[rows, :].astype(F32)
        conv_t[:, rows] = conv.T.astype(BF16)
    exchange(lambda d: conv_t.at[sixteen(d)], conv_rx.at[sixteen(s)], conv_s, conv_r, s)
    conv_rx[sixteen(s), :] = conv_t[sixteen(s), :]
    ring_in = Gather(in_shard, whole_in, sems_in, at)
    ring_in.begin()
    in_step = ring_in.steps()
    exchange(lambda d: mix_t.at[sixteen(d)], mix_rx.at[sixteen(s)], mix_s, mix_r, s)
    mix_rx[sixteen(s), :] = mix_t[sixteen(s), :]
    for r in range(0, ROWS, WIDE):
        rows = pl.ds(r, WIDE)
        grad_outer[rows, :] = (acc[rows, :] * conv_output[rows, :].astype(F32)).astype(BF16)
    loaded(5, *range(7, 15))

    def filter_rows(j, _):
        other_f[sixteen(j), :] = filters[:, lanes_at(j)].astype(F32)
        return 0

    lax.fori_loop(0, OUTER, filter_rows, 0)
    spectra = Spectra(tables)

    def take_filter(i, _):
        spec_h[i] = spectra.forward(other_f, i)
        return 0

    lax.fori_loop(0, 4, take_filter, 0)
    next(in_step)
    lax.fori_loop(4, 8, take_filter, 0)
    outs.partials(product_t, upstream, 6, 8)
    out_step = outs.steps()
    next(in_step)

    arrived(lambda d: conv_rx.at[sixteen(d)], conv_s, conv_r, s)
    spread(conv_rx, conv_f)

    def take_mixed(i, _):
        spec = spectra.forward(conv_f, i)
        spec_g[i] = spec
        spectra.inverse(spec, spec_h[i], out_f, i)
        return 0

    lax.fori_loop(0, 3, take_mixed, 0)
    next(in_step)
    lax.fori_loop(3, 6, take_mixed, 0)
    next(in_step)
    lax.fori_loop(6, 8, take_mixed, 0)

    def gather_rows(n, _):
        for q in range(3):
            mixed_cols[sixteen(n), q * WIDE : (q + 1) * WIDE] = out_f[
                sixteen(3 * n + q), :
            ].astype(BF16)
        return 0

    lax.fori_loop(0, N_SEQ, gather_rows, 0)
    exchange(lambda d: mixed_cols.at[sixteen(d)], mixed_rx.at[sixteen(s)], back_s, back_r, s)
    mixed_rx[sixteen(s), :] = mixed_cols[sixteen(s), :]

    arrived(lambda d: mix_rx.at[sixteen(d)], mix_s, mix_r, s)
    spread(mix_rx, other_f)

    def take_long(i, _):
        spectra.inverse(spec_g[i], spectra.forward(other_f, i), out_f, i)
        return 0

    lax.fori_loop(0, 2, take_long, 0)
    next(in_step)
    lax.fori_loop(2, 5, take_long, 0)
    next(in_step)
    lax.fori_loop(5, 8, take_long, 0)
    next(in_step)

    arrived(lambda d: mixed_rx.at[sixteen(d)], back_s, back_r, s)

    edge_back = remote(
        grads.at[pl.ds(0, 8)],
        halo_back,
        halo_sem.at[2],
        halo_sem.at[3],
        "seq",
        (s + N_SEQ - 1) % N_SEQ,
    )
    for r in range(0, ROWS, WIDE):
        rows = pl.ds(r, WIDE)
        mixed = mixed_rx[:, rows].astype(F32).T
        grads[rows, :] = mixed * gate[rows, :].astype(F32)
        if r == 0:
            edge_back.start()
        grad_inner[rows, :] = (mixed * smooth_rows(r)).astype(BF16)
    edge_back.wait_recv()
    grads[pl.ds(ROWS, 8), :] = jnp.where(s == N_SEQ - 1, 0.0, halo_back[...])
    for r in range(0, ROWS, WIDE):
        rows = pl.ds(r, WIDE)
        out = all_taps[pl.ds(0, 1), :] * grads[rows, :]
        for j in range(1, 3):
            out = out + all_taps[pl.ds(j, 1), :] * grads[pl.ds(r + j, WIDE), :]
        value[rows, :] = out.astype(BF16)
        value_t[:, rows] = out.T.astype(BF16)

    for _ in in_step:
        pass
    for sub in range(2):
        for o in range(-3, 5):
            ring_in.ready(sub, o)

    def part_of(sub, o):
        n = (1 - low if sub else low) * 4 + (x + o + 4) % 4
        w = jnp.concatenate([whole_in[4 * n + i] for i in range(4)], axis=0)
        acc[...] = lax.dot_general(
            value[...], w, (((1,), (1,)), ((), ())), preferred_element_type=F32
        )

    def x_hop(di, d, sub):
        return remote(
            x_own.at[sub, (SIGNS[di] * d) % 4],
            x_rx.at[di, d - 1, sub],
            x_s.at[di, d - 1, sub],
            x_r.at[di, d - 1, sub],
            "ch",
            low * 4 + (x + SIGNS[di] + 4) % 4,
        )

    hops = []

    def x_go(di, d, sub):
        o = (SIGNS[di] * d) % 4
        part_of(sub, o)
        value_out = acc[...]
        if d == 1 and sub == di:
            x_hop(di, 2, sub).wait_recv()
            value_out = value_out + x_rx[di, 1, sub].astype(F32)
        x_own[sub, o] = value_out.astype(BF16)
        hop = x_hop(di, d, sub)
        hop.start()
        hops.append(hop)

    def x_total(sub):
        part_of(sub, 0)
        value_out = acc[...]
        for di in range(2):
            x_hop(di, 1, sub).wait_recv()
            value_out = value_out + x_rx[di, 0, sub].astype(F32)
        return value_out

    partner = remote(y_io.at[0], y_io.at[1], p_s.at[0], p_s.at[1], "ch", (1 - low) * 4 + x)

    x_go(0, 2, 0)
    x_go(1, 2, 1)
    next(out_step)
    next(out_step)
    loaded(6)
    total = Scatter(scatter_in, at)
    total.partials(value_t, layer_input, 0, 2)
    step = total.steps()
    next(step)
    next(step)
    total.partials(value_t, layer_input, 2, 5)
    next(out_step)
    x_go(0, 1, 1)
    total.partials(value_t, layer_input, 5, 8)
    next(step)

    sums = []
    for j in range(3):
        part = jnp.zeros((1, CHANS), F32)
        for r in range(0, ROWS, WIDE):
            part = part + jnp.sum(
                grads[pl.ds(r, WIDE), :] * padded[pl.ds(8 + r - j, WIDE), :], axis=0, keepdims=True
            )
        sums.append(part)
    short_tx[...] = jnp.concatenate(sums + [jnp.zeros((5, CHANS), F32)], axis=0)
    exchange(lambda d: short_tx.at[:, lanes_at(d // 8)], short_rx.at[s], short_s, short_r, s)
    short_rx[s] = short_tx[:, lanes_at(s // 8)]

    x_go(1, 1, 1)
    next(step)
    next(out_step)

    def long_rows(j, _):
        grad_long[:, lanes_at(j)] = out_f[sixteen(j), :]
        return 0

    lax.fori_loop(0, OUTER, long_rows, 0)
    x_go(1, 1, 0)
    next(step)
    next(out_step)
    x_go(0, 1, 0)
    next(step)
    next(out_step)
    next(step)
    for _ in out_step:
        pass
    for _ in step:
        pass
    y_io[0] = x_total(1).astype(BF16)
    partner.start()
    outs.finish(grad_outproj)
    total.finish(inproj_t)
    grad_inproj[...] = inproj_t[...].T
    arrived(lambda d: short_rx.at[d], short_s, short_r, s)
    tile = short_rx[0]
    for i in range(1, N_SEQ):
        tile = tile + short_rx[i]
    grad_short[...] = tile
    edge_back.wait_send()
    grads[pl.ds(0, ROWS), :] = x_total(0)
    partner.wait_recv()
    grad_input[...] = (grads[pl.ds(0, ROWS), :] + y_io[1].astype(F32)).astype(BF16)

    for hop in hops:
        hop.wait_send()
    partner.wait_send()
    edge.wait_send()
    ring.end()
    ring_in.end()

    left(taps, taps_s, taps_r, s)
    left(mix_t.at[sixteen(0)], mix_s, mix_r, s)
    left(conv_t.at[sixteen(0)], conv_s, conv_r, s)
    left(mixed_cols.at[sixteen(0)], back_s, back_r, s)
    left(short_rx.at[0], short_s, short_r, s)


def hand_out(*refs):
    n = (len(refs) - 1) // 3
    sems = refs[-1]
    inward = [pltpu.make_async_copy(refs[i], refs[2 * n + i], sems.at[i]) for i in range(n)]
    outward = [
        pltpu.make_async_copy(refs[2 * n + i], refs[n + i], sems.at[n + i]) for i in range(n)
    ]
    for copy in inward:
        copy.start()
    for i in range(n):
        inward[i].wait()
        outward[i].start()
    for copy in outward:
        copy.wait()


def shards(
    layer_input, value_proj, outer_gate, inner_gate, conv_output,
    upstream, in_weight, out_weight, long_filter, short_filter,
):
    s = lax.axis_index("seq")
    dma = pltpu.SemaphoreType.DMA
    peers = dma((N_SEQ,))
    vmem = pltpu.VMEM
    lane = ((s % 8) * MINE).astype(jnp.int32)
    taps = lax.dynamic_update_slice(
        jnp.zeros((8, WIDE), F32), short_filter[0].T, (jnp.int32(0), lane)
    )
    tables = [jnp.asarray(t) for t in dft_tables()]
    outs = [
        jax.ShapeDtypeStruct(shape, dtype)
        for shape, dtype in (
            ((ROWS, CHANS), BF16),
            ((ROWS, CHANS), BF16),
            ((ROWS, CHANS), BF16),
            ((MINE, LENGTH), F32),
            ((8, WIDE), F32),
            ((WIDE, CHANS), F32),
            ((CHANS, WIDE), F32),
        )
    ]
    args = (
        layer_input, value_proj, outer_gate, inner_gate, conv_output, upstream, in_weight, out_weight,
        long_filter[0], taps, *tables,
    )
    local = [vmem((ROWS, CHANS), BF16)] * 4
    block = vmem((CHANS, ROWS), BF16)
    signal = vmem((MINE * OUTER, WIDE), F32)
    spectrum = vmem((MINE // 2, 2 * OUTER, 2 * WIDE), F32)
    scratch = [
        vmem((ROWS, DEEP), BF16),
        *local,
        vmem((ROWS, DEEP), BF16),
        vmem((MINE, LENGTH), BF16),
        *[vmem(t.shape, t.dtype) for t in tables],
        vmem((N_SEQ, CHANS, WIDE), BF16),
        vmem((N_SEQ, WIDE, CHANS), BF16),
        vmem((ROWS, CHANS), F32),
        *[block] * 7,
        vmem((ROWS, CHANS), BF16),
        block,
        vmem((2, 4, ROWS, CHANS), BF16),
        vmem((2, 2, 2, ROWS, CHANS), BF16),
        vmem((2, ROWS, CHANS), BF16),
        vmem((ROWS + 8, CHANS), F32),
        vmem((8, CHANS), F32),
        vmem((16, CHANS), BF16),
        vmem((N_SEQ, 8, WIDE), F32),
        vmem((ROWS + 8, CHANS), F32),
        vmem((8, CHANS), F32),
        vmem((8, CHANS), F32),
        vmem((N_SEQ, 8, WIDE), F32),
        signal, signal, signal, spectrum, spectrum,
        vmem((CHANS, WIDE), F32),
        dma((16,)), dma((5,)),
        *[peers] * 10,
        dma((2, 2, 2)), dma((2, 2, 2)), dma((2,)),
        *Gather.sems, *Gather.sems, *Scatter.scratch(), *Scatter.scratch(),
    ]
    results = pl.pallas_call(
        whole_kernel,
        out_shape=outs,
        in_specs=[pl.BlockSpec(memory_space=pl.ANY)] * len(args),
        out_specs=[pl.BlockSpec(memory_space=pltpu.VMEM)] * len(outs),
        scratch_shapes=scratch,
        compiler_params=pltpu.CompilerParams(
            collective_id=0, has_side_effects=True, vmem_limit_bytes=60 * 2**20
        ),
        cost_estimate=pl.CostEstimate(
            flops=12 * 10**9, bytes_accessed=20 * 2**20, transcendentals=0
        ),
    )(*args)
    (
        grad_input, grad_outer, grad_inner, grad_long, grad_short, grad_inproj, grad_outproj,
    ) = pl.pallas_call(
        hand_out,
        out_shape=outs,
        in_specs=[pl.BlockSpec(memory_space=pl.ANY)] * len(outs),
        out_specs=[pl.BlockSpec(memory_space=pl.ANY)] * len(outs),
        scratch_shapes=[*[vmem(o.shape, o.dtype) for o in outs], dma((2 * len(outs),))],
    )(*results)
    grad_taps = lax.dynamic_slice(grad_short, (jnp.int32(0), lane), (3, MINE)).T
    return (
        grad_input,
        grad_outer,
        grad_inner,
        grad_long[None],
        grad_taps[None],
        grad_inproj,
        grad_outproj,
    )


def solution(mesh):
    in_specs = (
        P("seq", None),
        P("seq", "ch"),
        P("seq", "ch"),
        P("seq", "ch"),
        P("seq", "ch"),
        P("seq", None),
        P("seq", "ch"),
        P("ch", "seq"),
        P("ch", "seq", None),
        P("ch", "seq", None),
    )
    out_specs = (
        P("seq", "ch"),
        P("seq", "ch"),
        P("seq", "ch"),
        P("ch", "seq", None),
        P("ch", "seq", None),
        P("seq", "ch"),
        P("ch", "seq"),
    )
    return jax.shard_map(shards, mesh=mesh, in_specs=in_specs, out_specs=out_specs, check_vma=False)
```

```python
import math

import ml_dtypes
import numpy as np
import jax
import jax.numpy as jnp
from jax import lax
from jax.experimental import pallas as pl
from jax.experimental.pallas import tpu as pltpu
from jax.sharding import PartitionSpec as P

MESH = pl.DeviceIdType.MESH
F32 = jnp.float32
BF16 = jnp.bfloat16
N_SEQ = 32
ROWS = 384
CHANS = 512
MINE = 16
WIDE = 128
DEEP = 4096
LENGTH = N_SEQ * ROWS
OUTER = LENGTH // WIDE
SIGNS = (1, -1)


def split_table(table):
    high = table.astype(ml_dtypes.bfloat16)
    low = (table - high.astype(np.float64)).astype(ml_dtypes.bfloat16)
    return high, low


def dft_tables():
    a = np.arange(OUTER)
    b = np.arange(WIDE)
    k1 = np.arange(OUTER)
    k2 = np.arange(WIDE)
    turn = np.pi / (2 * LENGTH)
    outer = 2 * np.pi * np.outer(k1, a) / OUTER + turn * WIDE * a[None, :]
    twist = 2 * np.pi * np.outer(k1, b) / LENGTH + turn * b[None, :]
    inner = 2 * np.pi * np.outer(b, k2) / WIDE
    first = np.concatenate([np.cos(outer), -np.sin(outer)], axis=0)
    co, si = np.cos(inner), np.sin(inner)
    second = np.block([[co, -si], [si, co]])
    third = np.block([[co, si], [-si, co]])
    last = np.concatenate([np.cos(outer).T, -np.sin(outer).T], axis=1) / LENGTH
    first_h, first_l = split_table(first)
    second_h, second_l = split_table(second)
    third_h, third_l = split_table(third)
    last_h, last_l = split_table(last)
    return (
        np.concatenate([first_h, first_l], axis=0),
        second_h,
        second_l,
        third_h,
        third_l,
        np.stack([last_h, last_l]),
        np.cos(twist).astype(np.float32),
        np.sin(twist).astype(np.float32),
    )


def remote_to(src, dst, send, recv, device):
    return pltpu.make_async_remote_copy(
        src_ref=src,
        dst_ref=dst,
        send_sem=send,
        recv_sem=recv,
        device_id=device,
        device_id_type=MESH,
    )


def remote(src, dst, send, recv, axis, index):
    return remote_to(src, dst, send, recv, {axis: index})


def place():
    s = lax.axis_index("seq")
    return s, s // 16, (s // 2) % 8, s % 2


def at_seq(y, z, c):
    return y * 16 + z * 2 + c


def greet_all(barrier, s):
    def body(i, _):
        pl.semaphore_signal(
            barrier, inc=1, device_id={"seq": (s + i) % N_SEQ}, device_id_type=MESH
        )
        return 0

    lax.fori_loop(1, N_SEQ, body, 0)


def exchange(source_of, target, sends, recvs, s):
    def body(i, _):
        dst = (s + i) % N_SEQ
        remote(source_of(dst), target, sends.at[i], recvs.at[i], "seq", dst).start()
        return 0

    lax.fori_loop(1, N_SEQ, body, 0)


def arrived(landing_of, sends, recvs, s):
    def body(i, _):
        src = (s + N_SEQ - i) % N_SEQ
        here = landing_of(src)
        remote(here, here, sends.at[i], recvs.at[i], "seq", src).wait_recv()
        return 0

    lax.fori_loop(1, N_SEQ, body, 0)


def left(piece, sends, recvs, s):
    def body(i, _):
        remote(piece, piece, sends.at[i], recvs.at[i], "seq", (s + i) % N_SEQ).wait_send()
        return 0

    lax.fori_loop(1, N_SEQ, body, 0)


OVER_Y = (0, 3, 5, 4)
EARLY_Y = (0, 1, 7, 4)


class Gather:
    sems = [
        pltpu.SemaphoreType.DMA((2, 4, 2)),
        pltpu.SemaphoreType.DMA((2, 4, 2)),
        pltpu.SemaphoreType.DMA((2, 8)),
        pltpu.SemaphoreType.DMA((2, 8)),
        pltpu.SemaphoreType.DMA((9,)),
    ]

    def __init__(self, shard, whole, sems, at):
        self.shard, self.whole, self.at = shard, whole, at
        self.half = shard.shape[0] // 2
        self.zs, self.zr, self.cs, self.cr, self.ys = sems
        self.started = []

    def slot(self, sub, o, other=False):
        _, y, z, c = self.at
        yy = 1 - y if sub else y
        return at_seq(yy, (z + o + 8) % 8, 1 - c if other else c)

    def go(self, copy):
        copy.start()
        self.started.append(copy)

    def source(self, sub, o):
        if sub == 0 and o == 0:
            return self.shard
        return self.whole.at[self.slot(sub, o)]

    def hop(self, di, d, sub):
        _, y, z, c = self.at
        o = -SIGNS[di] * (d - 1)
        src, dst = self.source(sub, o), self.whole.at[self.slot(sub, o)]
        if d == 4:
            rows = pl.ds(di * self.half, self.half)
            src = dst = self.whole.at[self.slot(sub, o), rows]
        self.go(
            remote(
                src,
                dst,
                self.zs.at[di, d - 1, sub],
                self.zr.at[di, d - 1, sub],
                "seq",
                at_seq(y, (z + SIGNS[di] + 8) % 8, c),
            )
        )

    def landed(self, di, d, sub):
        here = self.whole.at[self.slot(sub, -SIGNS[di] * d)]
        if d == 4:
            here = self.whole.at[self.slot(sub, 4), pl.ds(di * self.half, self.half)]
        remote(
            here, here, self.zs.at[di, d - 1, sub], self.zr.at[di, d - 1, sub], "seq", self.at[0]
        ).wait_recv()

    def share(self, sub, o):
        _, y, z, c = self.at
        self.go(
            remote(
                self.source(sub, o),
                self.whole.at[self.slot(sub, o)],
                self.cs.at[sub, o % 8],
                self.cr.at[sub, o % 8],
                "seq",
                at_seq(y, z, 1 - c),
            )
        )

    def over_y(self, n):
        _, y, z, c = self.at
        self.go(
            remote(
                self.source(0, EARLY_Y[n]),
                self.whole.at[self.slot(0, EARLY_Y[n])],
                self.ys.at[2 * n],
                self.ys.at[2 * n + 1],
                "seq",
                at_seq(1 - y, z, c),
            )
        )

    def from_y(self, n):
        here = self.whole.at[self.slot(1, EARLY_Y[n])]
        remote(
            here, here, self.ys.at[2 * n], self.ys.at[2 * n + 1], "seq", self.at[0]
        ).wait_recv()
        self.share(1, EARLY_Y[n])

    def begin(self):
        self.hop(0, 1, 0)
        self.hop(1, 1, 0)
        self.over_y(0)
        self.share(0, 0)
        self.keep = pltpu.make_async_copy(
            self.shard, self.whole.at[self.slot(0, 0)], self.ys.at[8]
        )
        self.keep.start()

    def serve(self, d, sub, on):
        for di in range(2):
            self.landed(di, d, sub)
            if on:
                self.hop(di, d + 1, sub)
        for di in range(2):
            if d < 4:
                self.share(sub, -SIGNS[di] * d)

    def steps(self):
        self.serve(1, 0, True)
        self.over_y(1)
        self.over_y(2)
        yield
        self.from_y(0)
        yield
        self.serve(2, 0, True)
        yield
        self.from_y(1)
        self.hop(1, 2, 1)
        self.from_y(2)
        self.hop(0, 2, 1)
        yield
        self.serve(3, 0, True)
        yield
        self.serve(2, 1, True)
        yield
        self.serve(4, 0, False)
        self.over_y(3)
        self.share(0, 4)
        yield
        self.serve(3, 1, False)
        yield
        self.from_y(3)
        yield

    def ready(self, sub, o):
        _, y, z, c = self.at
        if (sub, o) == (0, 0):
            self.keep.wait()
        here = self.whole.at[self.slot(sub, o, other=True)]
        remote(
            here, here, self.cs.at[sub, o % 8], self.cr.at[sub, o % 8], "seq", self.at[0]
        ).wait_recv()
        yy = 1 - y if sub else y
        return yy * 8 + (z + o + 8) % 8

    def end(self):
        for copy in self.started:
            copy.wait_send()


class Scatter:
    @staticmethod
    def scratch():
        return [
            pltpu.VMEM((2, 8, CHANS, WIDE), BF16),
            pltpu.VMEM((2, 8, CHANS, WIDE), BF16),
            pltpu.VMEM((2, 8, CHANS, WIDE), BF16),
            pltpu.VMEM((2, 4, 2, CHANS, WIDE), BF16),
            pltpu.VMEM((4, CHANS, WIDE), BF16),
            pltpu.SemaphoreType.DMA((2, 4, 2)),
            pltpu.SemaphoreType.DMA((2, 4, 2)),
            pltpu.SemaphoreType.DMA((2, 8)),
            pltpu.SemaphoreType.DMA((2, 8)),
            pltpu.SemaphoreType.DMA((8,)),
        ]

    def __init__(self, scratch, at):
        self.at = at
        self.own, self.tx, self.rx, self.zrx, self.yrx = scratch[:5]
        self.zs, self.zr, self.cs, self.cr, self.ys = scratch[5:]
        self.started = []

    def go(self, copy):
        copy.start()
        self.started.append(copy)

    def hand(self, sub, o):
        _, y, z, c = self.at
        return remote(
            self.tx.at[sub, o],
            self.rx.at[sub, o],
            self.cs.at[sub, o],
            self.cr.at[sub, o],
            "seq",
            at_seq(y, z, 1 - c),
        )

    def partials(self, left_t, right, first=0, last=8):
        _, y, z, c = self.at

        def body(i, _):
            o = (4 + (1 - 2 * (i % 2)) * ((i + 1) // 2) + 8) % 8
            columns = []
            for sub in range(2):
                m = (1 - y if sub else y) * 8 + (z + o) % 8
                columns.append(right[:, pl.ds(pl.multiple_of(m * 2 * WIDE, 2 * WIDE), 2 * WIDE)])
            both = jnp.dot(
                left_t[...], jnp.concatenate(columns, axis=1), preferred_element_type=F32
            )
            for sub in range(2):
                low = both[:, 2 * sub * WIDE : (2 * sub + 1) * WIDE].astype(BF16)
                high = both[:, (2 * sub + 1) * WIDE : (2 * sub + 2) * WIDE].astype(BF16)
                self.tx[sub, o] = jnp.where(c == 0, high, low)
                self.hand(sub, o).start()
                self.own[sub, o] = jnp.where(c == 0, low, high)
            return 0

        lax.fori_loop(first, last, body, 0)

    def hop(self, di, d, sub):
        _, y, z, c = self.at
        o = (SIGNS[di] * d) % 8
        src, dst = self.own.at[sub, o], self.zrx.at[di, d - 1, sub]
        if d == 4:
            half = CHANS // 2
            src = self.own.at[sub, o, pl.ds(di * half, half)]
            dst = self.zrx.at[di, d - 1, sub, pl.ds(0, half)]
        return remote(
            src,
            dst,
            self.zs.at[di, d - 1, sub],
            self.zr.at[di, d - 1, sub],
            "seq",
            at_seq(y, (z + SIGNS[di] + 8) % 8, c),
        )

    def over_y(self, n):
        _, y, z, c = self.at
        return remote(
            self.own.at[1, OVER_Y[n]],
            self.yrx.at[n],
            self.ys.at[2 * n],
            self.ys.at[2 * n + 1],
            "seq",
            at_seq(1 - y, z, c),
        )

    def both(self, sub, o):
        self.hand(sub, o).wait_recv()
        return self.own[sub, o].astype(F32) + self.rx[sub, o].astype(F32)

    def with_y(self, n):
        total = self.both(0, OVER_Y[n])
        self.over_y(n).wait_recv()
        return total + self.yrx[n].astype(F32)

    def steps(self):
        for n in (3, 1, 2):
            o = OVER_Y[n]
            self.own[1, o] = self.both(1, o).astype(BF16)
            self.go(self.over_y(n))
        yield
        self.own[0, 4] = self.with_y(3).astype(BF16)
        self.go(self.hop(0, 4, 0))
        self.go(self.hop(1, 4, 0))
        yield
        half = CHANS // 2
        for d, sub in ((2, 1), (3, 0), (1, 1), (2, 0), (0, 1), (1, 0)):
            if d == 0:
                self.own[1, 0] = self.ended(1).astype(BF16)
                self.go(self.over_y(0))
                yield
                continue
            for di in range(2):
                o = (SIGNS[di] * d) % 8
                if d == 3:
                    total = self.with_y(1 + di)
                    self.hop(di, 4, 0).wait_recv()
                    parts = [total[:half], total[half:]]
                    parts[di] = parts[di] + self.zrx[di, 3, 0, :half].astype(F32)
                    total = jnp.concatenate(parts, axis=0)
                else:
                    total = self.both(sub, o)
                    if (d, sub) != (2, 1):
                        self.hop(di, d + 1, sub).wait_recv()
                        total = total + self.zrx[di, d, sub].astype(F32)
                self.own[sub, o] = total.astype(BF16)
                self.go(self.hop(di, d, sub))
            yield

    def ended(self, sub):
        value = self.both(sub, 0)
        for di in range(2):
            self.hop(di, 1, sub).wait_recv()
            value = value + self.zrx[di, 0, sub].astype(F32)
        return value

    def finish(self, out):
        out[...] = self.ended(0)
        self.over_y(0).wait_recv()
        out[...] += self.yrx[0].astype(F32)
        for copy in self.started:
            copy.wait_send()

        def body(i, _):
            for sub in range(2):
                self.hand(sub, i).wait_send()
            return 0

        lax.fori_loop(0, 8, body, 0)


def sixteen(index):
    return pl.ds(pl.multiple_of(index * MINE, MINE), MINE)


def halves(x):
    high = x.astype(BF16)
    return high, (x - high.astype(F32)).astype(BF16)


def dot(a, b):
    return jnp.dot(a, b, preferred_element_type=F32)


def dot_three(x, table_h, table_l):
    high, low = halves(x)
    return dot(high, table_h[...]) + dot(high, table_l[...]) + dot(low, table_h[...])


class Spectra:
    def __init__(self, tables):
        (
            self.first,
            self.second_h,
            self.second_l,
            self.third_h,
            self.third_l,
            self.last,
            self.cos_t,
            self.sin_t,
        ) = tables

    def forward(self, source, i):
        signals = jnp.concatenate(
            [source[pl.ds(2 * i + n, OUTER, stride=MINE), :] for n in range(2)], axis=1
        ).astype(BF16)
        both = dot(self.first[...], signals)
        both = both[: 2 * OUTER] + both[2 * OUTER :]
        cos, sin = self.cos_t[...], self.sin_t[...]
        rows = []
        for n in range(2):
            re = both[:OUTER, n * WIDE : (n + 1) * WIDE]
            im = both[OUTER:, n * WIDE : (n + 1) * WIDE]
            rows.append(jnp.concatenate([re * cos + im * sin, im * cos - re * sin], axis=1))
        return dot_three(jnp.concatenate(rows, axis=0), self.second_h, self.second_l)

    def inverse(self, later, earlier, target, i):
        a, b = later[:, :WIDE], later[:, WIDE:]
        c, d = earlier[:, :WIDE], earlier[:, WIDE:]
        spec = jnp.concatenate([a * c + b * d, b * c - a * d], axis=1)
        mid = dot_three(spec, self.third_h, self.third_l)
        cos, sin = self.cos_t[...], self.sin_t[...]
        turned = []
        for n in range(2):
            re = mid[n * OUTER : (n + 1) * OUTER, :WIDE]
            im = mid[n * OUTER : (n + 1) * OUTER, WIDE:]
            turned.append(jnp.concatenate([re * cos - im * sin, im * cos + re * sin], axis=0))
        high, low = halves(jnp.concatenate(turned, axis=1))
        result = dot(self.last[0], high) + dot(self.last[1], high) + dot(self.last[0], low)
        for n in range(2):
            target[pl.ds(2 * i + n, OUTER, stride=MINE), :] = result[
                :, n * WIDE : (n + 1) * WIDE
            ]


def spread(cols, target):
    def body(s, _):
        for q in range(3):
            target[sixteen(3 * s + q), :] = cols[sixteen(s), q * WIDE : (q + 1) * WIDE].astype(F32)
        return 0

    lax.fori_loop(0, N_SEQ, body, 0)


def lanes_at(index):
    return pl.ds(pl.multiple_of(index * WIDE, WIDE), WIDE)


def whole_kernel(*refs):
    (
        layer_hbm, value_hbm, outer_hbm, gate_hbm, conv_hbm, up_hbm, in_shard, out_shard, filter_hbm, taps,
        *table_hbm,
    ) = refs[:18]
    (
        grad_input, grad_outer, grad_inner, grad_long, grad_short, grad_inproj, grad_outproj,
    ) = refs[18:25]
    (
        layer_input, value_in, outer_gate, gate, conv_output, upstream, filters, *tables,
    ) = refs[25:40]
    (
        whole_out, whole_in, acc, product_t, conv_t, mix_t, conv_rx, mix_rx, mixed_cols, mixed_rx,
        value, value_t, blocks, padded, all_taps, halo, taps_rx, grads, halo_back, short_tx, short_rx,
        conv_f, other_f, out_f, spec_g, spec_h, in_piece, inproj_t,
        load_sem, halo_sem, twin_sem, taps_s, taps_r, mix_s, mix_r, conv_s, conv_r,
        back_s, back_r, short_s, short_r, x_s, x_r, p_s,
    ) = refs[40:84]
    rest = refs[84:]
    sems_out, sems_in = rest[:5], rest[5:10]
    scatter_out, scatter_in = rest[10:20], rest[20:30]

    at = place()
    s, y, z, c = at
    ch = lax.axis_index("ch")
    x, low = ch % 4, ch // 4
    twin = {"seq": 4 * ch + s % 4, "ch": s // 4}
    away = s // 4 != ch

    barrier = pltpu.get_barrier_semaphore()
    greet_all(barrier, s)
    for there in (low * 4 + (x + 1) % 4, low * 4 + (x + 3) % 4, (1 - low) * 4 + x):
        pl.semaphore_signal(barrier, inc=1, device_id={"ch": there}, device_id_type=MESH)

    @pl.when(away)
    def _():
        pl.semaphore_signal(barrier, inc=1, device_id=twin, device_id_type=MESH)

    sources = [outer_hbm, conv_hbm, value_hbm, gate_hbm, up_hbm, filter_hbm, layer_hbm, *table_hbm]
    targets = [outer_gate, conv_output, value_in, gate, upstream, filters, layer_input, *tables]
    loads = {}
    for n, (src, dst) in enumerate(zip(sources, targets)):
        copy = pltpu.make_async_copy(src, dst, load_sem.at[n])
        copy.start()
        loads[n] = copy

    def loaded(*which):
        for n in which:
            loads[n].wait()

    @pl.when(away)
    def _():
        pl.semaphore_wait(barrier, N_SEQ - 1 + 4)

    @pl.when(jnp.logical_not(away))
    def _():
        pl.semaphore_wait(barrier, N_SEQ - 1 + 3)

    ring = Gather(out_shard, whole_out, sems_out, at)
    ring.begin()
    edge = remote(
        value_hbm.at[pl.ds(ROWS - 16, 16)],
        halo,
        halo_sem.at[0],
        halo_sem.at[1],
        "seq",
        (s + 1) % N_SEQ,
    )
    edge.start()
    exchange(lambda d: taps, taps_rx.at[s], taps_s, taps_r, s)
    taps_own = pltpu.make_async_copy(taps, taps_rx.at[s], halo_sem.at[4])
    taps_own.start()
    turn = remote_to(in_shard, in_piece, twin_sem.at[0], twin_sem.at[1], twin)
    stay = pltpu.make_async_copy(in_shard, in_piece, twin_sem.at[2])

    def turn_out():
        @pl.when(away)
        def _():
            turn.start()

        @pl.when(jnp.logical_not(away))
        def _():
            stay.start()

    step = ring.steps()
    loaded(0, 1)
    for r in range(0, ROWS, WIDE):
        rows = pl.ds(r, WIDE)
        product = outer_gate[rows, :].astype(F32) * conv_output[rows, :].astype(F32)
        product_t[:, rows] = product.T.astype(BF16)
    next(step)

    loaded(2, 3)
    for r in range(0, ROWS, WIDE):
        padded[pl.ds(8 + r, WIDE), :] = value_in[pl.ds(r, WIDE), :].astype(F32)
    arrived(lambda d: taps_rx.at[d], taps_s, taps_r, s)
    taps_own.wait()
    for g in range(4):
        tile = taps_rx[8 * g]
        for i in range(1, 8):
            tile = tile + taps_rx[8 * g + i]
        all_taps[:, pl.ds(g * WIDE, WIDE)] = tile
    edge.wait_recv()
    padded[pl.ds(0, 8), :] = jnp.where(s == 0, 0.0, halo[...].astype(F32)[8:, :])
    next(step)

    def smooth_rows(r):
        smooth = all_taps[pl.ds(0, 1), :] * padded[pl.ds(8 + r, WIDE), :]
        for j in range(1, 3):
            smooth = smooth + all_taps[pl.ds(j, 1), :] * padded[pl.ds(8 + r - j, WIDE), :]
        return smooth

    for r in range(0, ROWS, WIDE):
        mixed = gate[pl.ds(r, WIDE), :].astype(F32) * smooth_rows(r)
        mix_t[:, pl.ds(r, WIDE)] = mixed.T.astype(BF16)
    outs = Scatter(scatter_out, at)
    next(step)

    def multiply(sub, o, first=False):
        m = ring.ready(sub, o)
        cols = pl.ds(pl.multiple_of(m * 2 * WIDE, 2 * WIDE), 2 * WIDE)
        shards = jnp.concatenate([whole_out[2 * m], whole_out[2 * m + 1]], axis=1)
        part = lax.dot_general(
            upstream[:, cols], shards, (((1,), (1,)), ((), ())), preferred_element_type=F32
        )
        acc[...] = part if first else acc[...] + part

    loaded(4)
    multiply(0, 0, True)
    multiply(0, 1)
    multiply(0, -1)
    outs.partials(product_t, upstream, 0, 1)
    order = ((1, (0,)), (0, (2, -2)), (1, (1, -1)), (0, (3, -3)), (1, (2, -2)), (0, (4,)))
    for n, (sub, offsets) in enumerate(order):
        next(step)
        if n == 1:
            turn_out()
        for o in offsets:
            multiply(sub, o)
        if n < 5:
            outs.partials(product_t, upstream, n + 1, n + 2)
    multiply(1, 3)
    multiply(1, -3)
    for _ in step:
        pass
    multiply(1, 4)

    for r in range(0, ROWS, WIDE):
        rows = pl.ds(r, WIDE)
        conv = acc[rows, :] * outer_gate[rows, :].astype(F32)
        conv_t[:, rows] = conv.T.astype(BF16)
    exchange(lambda d: conv_t.at[sixteen(d)], conv_rx.at[sixteen(s)], conv_s, conv_r, s)
    conv_rx[sixteen(s), :] = conv_t[sixteen(s), :]

    @pl.when(away)
    def _():
        turn.wait_recv()

    @pl.when(jnp.logical_not(away))
    def _():
        stay.wait()

    ring_in = Gather(in_piece, whole_in, sems_in, at)
    ring_in.begin()
    in_step = ring_in.steps()
    for r in range(0, ROWS, WIDE):
        rows = pl.ds(r, WIDE)
        grad_outer[rows, :] = (acc[rows, :] * conv_output[rows, :].astype(F32)).astype(BF16)
    loaded(5, *range(7, 15))

    def filter_rows(j, _):
        other_f[sixteen(j), :] = filters[:, lanes_at(j)].astype(F32)
        return 0

    lax.fori_loop(0, OUTER, filter_rows, 0)
    spectra = Spectra(tables)

    def take_filter(i, _):
        spec_h[i] = spectra.forward(other_f, i)
        return 0

    lax.fori_loop(0, 4, take_filter, 0)
    next(in_step)
    lax.fori_loop(4, 8, take_filter, 0)
    outs.partials(product_t, upstream, 6, 8)
    out_step = outs.steps()
    next(out_step)
    next(in_step)

    arrived(lambda d: conv_rx.at[sixteen(d)], conv_s, conv_r, s)
    exchange(lambda d: mix_t.at[sixteen(d)], mix_rx.at[sixteen(s)], mix_s, mix_r, s)
    mix_rx[sixteen(s), :] = mix_t[sixteen(s), :]
    spread(conv_rx, conv_f)

    def take_mixed(i, _):
        spec = spectra.forward(conv_f, i)
        spec_g[i] = spec
        spectra.inverse(spec, spec_h[i], out_f, i)
        return 0

    lax.fori_loop(0, 3, take_mixed, 0)
    next(in_step)
    lax.fori_loop(3, 6, take_mixed, 0)
    next(in_step)
    lax.fori_loop(6, 8, take_mixed, 0)

    def gather_rows(n, _):
        for q in range(3):
            mixed_cols[sixteen(n), q * WIDE : (q + 1) * WIDE] = out_f[
                sixteen(3 * n + q), :
            ].astype(BF16)
        return 0

    lax.fori_loop(0, N_SEQ, gather_rows, 0)
    exchange(lambda d: mixed_cols.at[sixteen(d)], mixed_rx.at[sixteen(s)], back_s, back_r, s)
    mixed_rx[sixteen(s), :] = mixed_cols[sixteen(s), :]

    def take_long(i, _):
        spectra.inverse(spec_g[i], spectra.forward(other_f, i), out_f, i)
        return 0

    next(in_step)
    arrived(lambda d: mix_rx.at[sixteen(d)], mix_s, mix_r, s)
    spread(mix_rx, other_f)
    lax.fori_loop(0, 3, take_long, 0)
    next(in_step)
    lax.fori_loop(3, 6, take_long, 0)
    next(in_step)
    arrived(lambda d: mixed_rx.at[sixteen(d)], back_s, back_r, s)
    next(out_step)
    next(out_step)

    edge_back = remote(
        grads.at[pl.ds(0, 8)],
        halo_back,
        halo_sem.at[2],
        halo_sem.at[3],
        "seq",
        (s + N_SEQ - 1) % N_SEQ,
    )
    for r in range(0, ROWS, WIDE):
        rows = pl.ds(r, WIDE)
        mixed = mixed_rx[:, rows].astype(F32).T
        grads[rows, :] = mixed * gate[rows, :].astype(F32)
        if r == 0:
            edge_back.start()
        grad_inner[rows, :] = (mixed * smooth_rows(r)).astype(BF16)
    edge_back.wait_recv()
    grads[pl.ds(ROWS, 8), :] = jnp.where(s == N_SEQ - 1, 0.0, halo_back[...])
    for r in range(0, ROWS, WIDE):
        rows = pl.ds(r, WIDE)
        out = all_taps[pl.ds(0, 1), :] * grads[rows, :]
        for j in range(1, 3):
            out = out + all_taps[pl.ds(j, 1), :] * grads[pl.ds(r + j, WIDE), :]
        value[rows, :] = out.astype(BF16)
        value_t[:, rows] = out.T.astype(BF16)

    def block(sub, o):
        return (1 - low if sub else low) * 4 + (x + o + 4) % 4

    def x_hop(di, d, sub):
        o = -SIGNS[di] * (d - 1)
        return remote(
            value if (sub, o) == (0, 0) else blocks.at[block(sub, o)],
            blocks.at[block(sub, o)],
            x_s.at[di, d - 1, sub],
            x_r.at[di, d - 1, sub],
            "ch",
            low * 4 + (x + SIGNS[di] + 4) % 4,
        )

    def x_wait(di, d, sub):
        here = blocks.at[block(sub, -SIGNS[di] * d)]
        remote(
            here, here, x_s.at[di, d - 1, sub], x_r.at[di, d - 1, sub], "ch", ch
        ).wait_recv()

    partner = remote(
        value, blocks.at[block(0, 0)], p_s.at[0], p_s.at[1], "ch", (1 - low) * 4 + x
    )
    hops = []

    def x_go(di, d, sub):
        hop = x_hop(di, d, sub)
        hop.start()
        hops.append(hop)

    x_go(0, 1, 0)
    x_go(1, 1, 0)
    partner.start()
    next(out_step)
    blocks[block(0, 0)] = value[...]
    loaded(6)
    total = Scatter(scatter_in, at)
    total.partials(value_t, layer_input, 0, 3)
    step = total.steps()
    next(step)
    total.partials(value_t, layer_input, 3, 6)
    next(step)
    next(out_step)
    total.partials(value_t, layer_input, 6, 8)
    next(step)
    partner.wait_recv()
    x_go(0, 1, 1)
    x_go(1, 1, 1)
    next(step)
    next(out_step)

    sums = []
    for j in range(3):
        part = jnp.zeros((1, CHANS), F32)
        for r in range(0, ROWS, WIDE):
            part = part + jnp.sum(
                grads[pl.ds(r, WIDE), :] * padded[pl.ds(8 + r - j, WIDE), :], axis=0, keepdims=True
            )
        sums.append(part)
    short_tx[...] = jnp.concatenate(sums + [jnp.zeros((5, CHANS), F32)], axis=0)
    exchange(lambda d: short_tx.at[:, lanes_at(d // 8)], short_rx.at[s], short_s, short_r, s)
    short_rx[s] = short_tx[:, lanes_at(s // 8)]

    x_wait(0, 1, 0)
    x_go(0, 2, 0)
    x_wait(1, 1, 0)
    next(step)
    next(out_step)
    next(in_step)
    next(step)
    next(out_step)
    next(in_step)
    x_wait(1, 1, 1)
    x_go(1, 2, 1)
    next(step)
    for _ in out_step:
        pass
    for _ in in_step:
        pass
    lax.fori_loop(6, 8, take_long, 0)
    next(step)

    def long_rows(j, _):
        grad_long[:, lanes_at(j)] = out_f[sixteen(j), :]
        return 0

    lax.fori_loop(0, OUTER, long_rows, 0)
    for sub in range(2):
        for o in range(-3, 5):
            ring_in.ready(sub, o)

    def finish(n, first=False):
        w = jnp.concatenate([whole_in[4 * n + i] for i in range(4)], axis=0)
        part = lax.dot_general(
            blocks[n], w, (((1,), (1,)), ((), ())), preferred_element_type=F32
        )
        acc[...] = part if first else acc[...] + part

    finish(ch, True)
    finish(block(1, 0))
    finish(block(0, -1))
    finish(block(0, 1))
    finish(block(1, 1))
    for _ in step:
        pass
    outs.finish(grad_outproj)
    x_wait(0, 1, 1)
    finish(block(1, -1))
    total.finish(inproj_t)
    grad_inproj[...] = inproj_t[...].T
    arrived(lambda d: short_rx.at[d], short_s, short_r, s)
    tile = short_rx[0]
    for i in range(1, N_SEQ):
        tile = tile + short_rx[i]
    grad_short[...] = tile
    x_wait(0, 2, 0)
    finish(block(0, 2))
    x_wait(1, 2, 1)
    finish(block(1, 2))
    grad_input[...] = acc[...].astype(BF16)
    edge_back.wait_send()

    for hop in hops:
        hop.wait_send()
    partner.wait_send()
    edge.wait_send()
    ring.end()
    ring_in.end()

    @pl.when(away)
    def _():
        turn.wait_send()


    left(taps, taps_s, taps_r, s)
    left(mix_t.at[sixteen(0)], mix_s, mix_r, s)
    left(conv_t.at[sixteen(0)], conv_s, conv_r, s)
    left(mixed_cols.at[sixteen(0)], back_s, back_r, s)
    left(short_rx.at[0], short_s, short_r, s)


def hand_out(*refs):
    n = (len(refs) - 1) // 3
    sems = refs[-1]
    inward = [pltpu.make_async_copy(refs[i], refs[2 * n + i], sems.at[i]) for i in range(n)]
    outward = [
        pltpu.make_async_copy(refs[2 * n + i], refs[n + i], sems.at[n + i]) for i in range(n)
    ]
    for copy in inward:
        copy.start()
    for i in range(n):
        inward[i].wait()
        outward[i].start()
    for copy in outward:
        copy.wait()


def shards(
    layer_input, value_proj, outer_gate, inner_gate, conv_output,
    upstream, in_weight, out_weight, long_filter, short_filter,
):
    s = lax.axis_index("seq")
    dma = pltpu.SemaphoreType.DMA
    peers = dma((N_SEQ,))
    vmem = pltpu.VMEM
    lane = ((s % 8) * MINE).astype(jnp.int32)
    taps = lax.dynamic_update_slice(
        jnp.zeros((8, WIDE), F32), short_filter[0].T, (jnp.int32(0), lane)
    )
    tables = [jnp.asarray(t) for t in dft_tables()]
    outs = [
        jax.ShapeDtypeStruct(shape, dtype)
        for shape, dtype in (
            ((ROWS, CHANS), BF16),
            ((ROWS, CHANS), BF16),
            ((ROWS, CHANS), BF16),
            ((MINE, LENGTH), F32),
            ((8, WIDE), F32),
            ((WIDE, CHANS), F32),
            ((CHANS, WIDE), F32),
        )
    ]
    args = (
        layer_input, value_proj, outer_gate, inner_gate, conv_output, upstream, in_weight, out_weight,
        long_filter[0], taps, *tables,
    )
    local = [vmem((ROWS, CHANS), BF16)] * 4
    block = vmem((CHANS, ROWS), BF16)
    signal = vmem((MINE * OUTER, WIDE), F32)
    spectrum = vmem((MINE // 2, 2 * OUTER, 2 * WIDE), F32)
    scratch = [
        vmem((ROWS, DEEP), BF16),
        *local,
        vmem((ROWS, DEEP), BF16),
        vmem((MINE, LENGTH), BF16),
        *[vmem(t.shape, t.dtype) for t in tables],
        vmem((N_SEQ, CHANS, WIDE), BF16),
        vmem((N_SEQ, WIDE, CHANS), BF16),
        vmem((ROWS, CHANS), F32),
        *[block] * 7,
        vmem((ROWS, CHANS), BF16),
        block,
        vmem((8, ROWS, CHANS), BF16),
        vmem((ROWS + 8, CHANS), F32),
        vmem((8, CHANS), F32),
        vmem((16, CHANS), BF16),
        vmem((N_SEQ, 8, WIDE), F32),
        vmem((ROWS + 8, CHANS), F32),
        vmem((8, CHANS), F32),
        vmem((8, CHANS), F32),
        vmem((N_SEQ, 8, WIDE), F32),
        signal, signal, signal, spectrum, spectrum,
        vmem((WIDE, CHANS), BF16),
        vmem((CHANS, WIDE), F32),
        dma((16,)), dma((5,)), dma((3,)),
        *[peers] * 10,
        dma((2, 2, 2)), dma((2, 2, 2)), dma((2,)),
        *Gather.sems, *Gather.sems, *Scatter.scratch(), *Scatter.scratch(),
    ]
    results = pl.pallas_call(
        whole_kernel,
        out_shape=outs,
        in_specs=[pl.BlockSpec(memory_space=pl.ANY)] * len(args),
        out_specs=[pl.BlockSpec(memory_space=pltpu.VMEM)] * len(outs),
        scratch_shapes=scratch,
        compiler_params=pltpu.CompilerParams(
            collective_id=0, has_side_effects=True, vmem_limit_bytes=60 * 2**20
        ),
        cost_estimate=pl.CostEstimate(
            flops=12 * 10**9, bytes_accessed=20 * 2**20, transcendentals=0
        ),
    )(*args)
    (
        grad_input, grad_outer, grad_inner, grad_long, grad_short, grad_inproj, grad_outproj,
    ) = pl.pallas_call(
        hand_out,
        out_shape=outs,
        in_specs=[pl.BlockSpec(memory_space=pl.ANY)] * len(outs),
        out_specs=[pl.BlockSpec(memory_space=pl.ANY)] * len(outs),
        scratch_shapes=[*[vmem(o.shape, o.dtype) for o in outs], dma((2 * len(outs),))],
    )(*results)
    grad_taps = lax.dynamic_slice(grad_short, (jnp.int32(0), lane), (3, MINE)).T
    return (
        grad_input,
        grad_outer,
        grad_inner,
        grad_long[None],
        grad_taps[None],
        grad_inproj,
        grad_outproj,
    )


def solution(mesh):
    in_specs = (
        P("seq", None),
        P("seq", "ch"),
        P("seq", "ch"),
        P("seq", "ch"),
        P("seq", "ch"),
        P("seq", None),
        P("seq", "ch"),
        P("ch", "seq"),
        P("ch", "seq", None),
        P("ch", "seq", None),
    )
    out_specs = (
        P("seq", "ch"),
        P("seq", "ch"),
        P("seq", "ch"),
        P("ch", "seq", None),
        P("ch", "seq", None),
        P("seq", "ch"),
        P("ch", "seq"),
    )
    return jax.shard_map(shards, mesh=mesh, in_specs=in_specs, out_specs=out_specs, check_vma=False)
```

```python
import math

import ml_dtypes
import numpy as np
import jax
import jax.numpy as jnp
from jax import lax
from jax.experimental import pallas as pl
from jax.experimental.pallas import tpu as pltpu
from jax.sharding import PartitionSpec as P

MESH = pl.DeviceIdType.MESH
F32 = jnp.float32
BF16 = jnp.bfloat16
N_SEQ = 32
ROWS = 384
CHANS = 512
MINE = 16
WIDE = 128
DEEP = 4096
LENGTH = N_SEQ * ROWS
OUTER = LENGTH // WIDE
SIGNS = (1, -1)


def split_table(table):
    high = table.astype(ml_dtypes.bfloat16)
    low = (table - high.astype(np.float64)).astype(ml_dtypes.bfloat16)
    return high, low


def dft_tables():
    a = np.arange(OUTER)
    b = np.arange(WIDE)
    k1 = np.arange(OUTER)
    k2 = np.arange(WIDE)
    turn = np.pi / (2 * LENGTH)
    outer = 2 * np.pi * np.outer(k1, a) / OUTER + turn * WIDE * a[None, :]
    twist = 2 * np.pi * np.outer(k1, b) / LENGTH + turn * b[None, :]
    inner = 2 * np.pi * np.outer(b, k2) / WIDE
    first = np.concatenate([np.cos(outer), -np.sin(outer)], axis=0)
    co, si = np.cos(inner), np.sin(inner)
    second = np.block([[co, -si], [si, co]])
    third = np.block([[co, si], [-si, co]])
    last = np.concatenate([np.cos(outer).T, -np.sin(outer).T], axis=1) / LENGTH
    first_h, first_l = split_table(first)
    second_h, second_l = split_table(second)
    third_h, third_l = split_table(third)
    last_h, last_l = split_table(last)
    return (
        np.concatenate([first_h, first_l], axis=0),
        second_h,
        second_l,
        third_h,
        third_l,
        np.stack([last_h, last_l]),
        np.cos(twist).astype(np.float32),
        np.sin(twist).astype(np.float32),
    )


def remote_to(src, dst, send, recv, device):
    return pltpu.make_async_remote_copy(
        src_ref=src,
        dst_ref=dst,
        send_sem=send,
        recv_sem=recv,
        device_id=device,
        device_id_type=MESH,
    )


def remote(src, dst, send, recv, axis, index):
    return remote_to(src, dst, send, recv, {axis: index})


def place():
    s = lax.axis_index("seq")
    return s, s // 16, (s // 2) % 8, s % 2


def at_seq(y, z, c):
    return y * 16 + z * 2 + c


def greet_all(barrier, s):
    def body(i, _):
        pl.semaphore_signal(
            barrier, inc=1, device_id={"seq": (s + i) % N_SEQ}, device_id_type=MESH
        )
        return 0

    lax.fori_loop(1, N_SEQ, body, 0)


def exchange(source_of, target, sends, recvs, s):
    def body(i, _):
        dst = (s + i) % N_SEQ
        remote(source_of(dst), target, sends.at[i], recvs.at[i], "seq", dst).start()
        return 0

    lax.fori_loop(1, N_SEQ, body, 0)


def arrived(landing_of, sends, recvs, s):
    def body(i, _):
        src = (s + N_SEQ - i) % N_SEQ
        here = landing_of(src)
        remote(here, here, sends.at[i], recvs.at[i], "seq", src).wait_recv()
        return 0

    lax.fori_loop(1, N_SEQ, body, 0)


def left(piece, sends, recvs, s):
    def body(i, _):
        remote(piece, piece, sends.at[i], recvs.at[i], "seq", (s + i) % N_SEQ).wait_send()
        return 0

    lax.fori_loop(1, N_SEQ, body, 0)


OVER_Y = (0, 3, 5, 4)
EARLY_Y = (0, 1, 7, 4)


class Gather:
    sems = [
        pltpu.SemaphoreType.DMA((2, 4, 2)),
        pltpu.SemaphoreType.DMA((2, 4, 2)),
        pltpu.SemaphoreType.DMA((2, 8)),
        pltpu.SemaphoreType.DMA((2, 8)),
        pltpu.SemaphoreType.DMA((9,)),
    ]

    def __init__(self, shard, whole, sems, at):
        self.shard, self.whole, self.at = shard, whole, at
        self.half = shard.shape[0] // 2
        self.zs, self.zr, self.cs, self.cr, self.ys = sems
        self.started = []

    def slot(self, sub, o, other=False):
        _, y, z, c = self.at
        yy = 1 - y if sub else y
        return at_seq(yy, (z + o + 8) % 8, 1 - c if other else c)

    def go(self, copy):
        copy.start()
        self.started.append(copy)

    def source(self, sub, o):
        if sub == 0 and o == 0:
            return self.shard
        return self.whole.at[self.slot(sub, o)]

    def hop(self, di, d, sub):
        _, y, z, c = self.at
        o = -SIGNS[di] * (d - 1)
        src, dst = self.source(sub, o), self.whole.at[self.slot(sub, o)]
        if d == 4:
            rows = pl.ds(di * self.half, self.half)
            src = dst = self.whole.at[self.slot(sub, o), rows]
        self.go(
            remote(
                src,
                dst,
                self.zs.at[di, d - 1, sub],
                self.zr.at[di, d - 1, sub],
                "seq",
                at_seq(y, (z + SIGNS[di] + 8) % 8, c),
            )
        )

    def landed(self, di, d, sub):
        here = self.whole.at[self.slot(sub, -SIGNS[di] * d)]
        if d == 4:
            here = self.whole.at[self.slot(sub, 4), pl.ds(di * self.half, self.half)]
        remote(
            here, here, self.zs.at[di, d - 1, sub], self.zr.at[di, d - 1, sub], "seq", self.at[0]
        ).wait_recv()

    def share(self, sub, o):
        _, y, z, c = self.at
        self.go(
            remote(
                self.source(sub, o),
                self.whole.at[self.slot(sub, o)],
                self.cs.at[sub, o % 8],
                self.cr.at[sub, o % 8],
                "seq",
                at_seq(y, z, 1 - c),
            )
        )

    def over_y(self, n):
        _, y, z, c = self.at
        self.go(
            remote(
                self.source(0, EARLY_Y[n]),
                self.whole.at[self.slot(0, EARLY_Y[n])],
                self.ys.at[2 * n],
                self.ys.at[2 * n + 1],
                "seq",
                at_seq(1 - y, z, c),
            )
        )

    def from_y(self, n):
        here = self.whole.at[self.slot(1, EARLY_Y[n])]
        remote(
            here, here, self.ys.at[2 * n], self.ys.at[2 * n + 1], "seq", self.at[0]
        ).wait_recv()
        self.share(1, EARLY_Y[n])

    def begin(self):
        self.hop(0, 1, 0)
        self.hop(1, 1, 0)
        self.over_y(0)
        self.share(0, 0)
        self.keep = pltpu.make_async_copy(
            self.shard, self.whole.at[self.slot(0, 0)], self.ys.at[8]
        )
        self.keep.start()

    def serve(self, d, sub, on):
        for di in range(2):
            self.landed(di, d, sub)
            if on:
                self.hop(di, d + 1, sub)
        for di in range(2):
            if d < 4:
                self.share(sub, -SIGNS[di] * d)

    def steps(self):
        self.serve(1, 0, True)
        self.over_y(1)
        self.over_y(2)
        yield
        self.from_y(0)
        yield
        self.serve(2, 0, True)
        yield
        self.from_y(1)
        self.hop(1, 2, 1)
        self.from_y(2)
        self.hop(0, 2, 1)
        yield
        self.serve(3, 0, True)
        yield
        self.serve(2, 1, True)
        yield
        self.serve(4, 0, False)
        self.over_y(3)
        self.share(0, 4)
        yield
        self.serve(3, 1, False)
        yield
        self.from_y(3)
        yield

    def ready(self, sub, o):
        _, y, z, c = self.at
        if (sub, o) == (0, 0):
            self.keep.wait()
        here = self.whole.at[self.slot(sub, o, other=True)]
        remote(
            here, here, self.cs.at[sub, o % 8], self.cr.at[sub, o % 8], "seq", self.at[0]
        ).wait_recv()
        yy = 1 - y if sub else y
        return yy * 8 + (z + o + 8) % 8

    def end(self):
        for copy in self.started:
            copy.wait_send()


class Scatter:
    @staticmethod
    def scratch():
        return [
            pltpu.VMEM((2, 8, CHANS, WIDE), BF16),
            pltpu.VMEM((2, 8, CHANS, WIDE), BF16),
            pltpu.VMEM((2, 8, CHANS, WIDE), BF16),
            pltpu.VMEM((2, 4, 2, CHANS, WIDE), BF16),
            pltpu.VMEM((4, CHANS, WIDE), BF16),
            pltpu.SemaphoreType.DMA((2, 4, 2)),
            pltpu.SemaphoreType.DMA((2, 4, 2)),
            pltpu.SemaphoreType.DMA((2, 8)),
            pltpu.SemaphoreType.DMA((2, 8)),
            pltpu.SemaphoreType.DMA((8,)),
        ]

    def __init__(self, scratch, at):
        self.at = at
        self.own, self.tx, self.rx, self.zrx, self.yrx = scratch[:5]
        self.zs, self.zr, self.cs, self.cr, self.ys = scratch[5:]
        self.started = []

    def go(self, copy):
        copy.start()
        self.started.append(copy)

    def hand(self, sub, o):
        _, y, z, c = self.at
        return remote(
            self.tx.at[sub, o],
            self.rx.at[sub, o],
            self.cs.at[sub, o],
            self.cr.at[sub, o],
            "seq",
            at_seq(y, z, 1 - c),
        )

    def partials(self, left_t, right, first=0, last=8):
        _, y, z, c = self.at

        def body(i, _):
            o = (4 + (1 - 2 * (i % 2)) * ((i + 1) // 2) + 8) % 8
            columns = []
            for sub in range(2):
                m = (1 - y if sub else y) * 8 + (z + o) % 8
                columns.append(right[:, pl.ds(pl.multiple_of(m * 2 * WIDE, 2 * WIDE), 2 * WIDE)])
            both = jnp.dot(
                left_t[...], jnp.concatenate(columns, axis=1), preferred_element_type=F32
            )
            for sub in range(2):
                low = both[:, 2 * sub * WIDE : (2 * sub + 1) * WIDE].astype(BF16)
                high = both[:, (2 * sub + 1) * WIDE : (2 * sub + 2) * WIDE].astype(BF16)
                self.tx[sub, o] = jnp.where(c == 0, high, low)
                self.hand(sub, o).start()
                self.own[sub, o] = jnp.where(c == 0, low, high)
            return 0

        lax.fori_loop(first, last, body, 0)

    def hop(self, di, d, sub):
        _, y, z, c = self.at
        o = (SIGNS[di] * d) % 8
        src, dst = self.own.at[sub, o], self.zrx.at[di, d - 1, sub]
        if d == 4:
            half = CHANS // 2
            src = self.own.at[sub, o, pl.ds(di * half, half)]
            dst = self.zrx.at[di, d - 1, sub, pl.ds(0, half)]
        return remote(
            src,
            dst,
            self.zs.at[di, d - 1, sub],
            self.zr.at[di, d - 1, sub],
            "seq",
            at_seq(y, (z + SIGNS[di] + 8) % 8, c),
        )

    def over_y(self, n):
        _, y, z, c = self.at
        return remote(
            self.own.at[1, OVER_Y[n]],
            self.yrx.at[n],
            self.ys.at[2 * n],
            self.ys.at[2 * n + 1],
            "seq",
            at_seq(1 - y, z, c),
        )

    def both(self, sub, o):
        self.hand(sub, o).wait_recv()
        return self.own[sub, o].astype(F32) + self.rx[sub, o].astype(F32)

    def with_y(self, n):
        total = self.both(0, OVER_Y[n])
        self.over_y(n).wait_recv()
        return total + self.yrx[n].astype(F32)

    def steps(self):
        for n in (3, 1, 2):
            o = OVER_Y[n]
            self.own[1, o] = self.both(1, o).astype(BF16)
            self.go(self.over_y(n))
        yield
        self.own[0, 4] = self.with_y(3).astype(BF16)
        self.go(self.hop(0, 4, 0))
        self.go(self.hop(1, 4, 0))
        yield
        half = CHANS // 2
        for d, sub in ((2, 1), (3, 0), (1, 1), (2, 0), (0, 1), (1, 0)):
            if d == 0:
                self.own[1, 0] = self.ended(1).astype(BF16)
                self.go(self.over_y(0))
                yield
                continue
            for di in range(2):
                o = (SIGNS[di] * d) % 8
                if d == 3:
                    total = self.with_y(1 + di)
                    self.hop(di, 4, 0).wait_recv()
                    parts = [total[:half], total[half:]]
                    parts[di] = parts[di] + self.zrx[di, 3, 0, :half].astype(F32)
                    total = jnp.concatenate(parts, axis=0)
                else:
                    total = self.both(sub, o)
                    if (d, sub) != (2, 1):
                        self.hop(di, d + 1, sub).wait_recv()
                        total = total + self.zrx[di, d, sub].astype(F32)
                self.own[sub, o] = total.astype(BF16)
                self.go(self.hop(di, d, sub))
            yield

    def ended(self, sub):
        value = self.both(sub, 0)
        for di in range(2):
            self.hop(di, 1, sub).wait_recv()
            value = value + self.zrx[di, 0, sub].astype(F32)
        return value

    def finish(self, out):
        out[...] = self.ended(0)
        self.over_y(0).wait_recv()
        out[...] += self.yrx[0].astype(F32)
        for copy in self.started:
            copy.wait_send()

        def body(i, _):
            for sub in range(2):
                self.hand(sub, i).wait_send()
            return 0

        lax.fori_loop(0, 8, body, 0)


def sixteen(index):
    return pl.ds(pl.multiple_of(index * MINE, MINE), MINE)


def halves(x):
    high = x.astype(BF16)
    return high, (x - high.astype(F32)).astype(BF16)


def dot(a, b):
    return jnp.dot(a, b, preferred_element_type=F32)


def dot_three(x, table_h, table_l):
    high, low = halves(x)
    return dot(high, table_h[...]) + dot(high, table_l[...]) + dot(low, table_h[...])


class Spectra:
    def __init__(self, tables):
        (
            self.first,
            self.second_h,
            self.second_l,
            self.third_h,
            self.third_l,
            self.last,
            self.cos_t,
            self.sin_t,
        ) = tables

    def forward(self, source, i):
        signals = jnp.concatenate(
            [source[pl.ds(2 * i + n, OUTER, stride=MINE), :] for n in range(2)], axis=1
        ).astype(BF16)
        both = dot(self.first[...], signals)
        both = both[: 2 * OUTER] + both[2 * OUTER :]
        cos, sin = self.cos_t[...], self.sin_t[...]
        rows = []
        for n in range(2):
            re = both[:OUTER, n * WIDE : (n + 1) * WIDE]
            im = both[OUTER:, n * WIDE : (n + 1) * WIDE]
            rows.append(jnp.concatenate([re * cos + im * sin, im * cos - re * sin], axis=1))
        return dot_three(jnp.concatenate(rows, axis=0), self.second_h, self.second_l)

    def inverse(self, later, earlier, target, i):
        a, b = later[:, :WIDE], later[:, WIDE:]
        c, d = earlier[:, :WIDE], earlier[:, WIDE:]
        spec = jnp.concatenate([a * c + b * d, b * c - a * d], axis=1)
        mid = dot_three(spec, self.third_h, self.third_l)
        cos, sin = self.cos_t[...], self.sin_t[...]
        turned = []
        for n in range(2):
            re = mid[n * OUTER : (n + 1) * OUTER, :WIDE]
            im = mid[n * OUTER : (n + 1) * OUTER, WIDE:]
            turned.append(jnp.concatenate([re * cos - im * sin, im * cos + re * sin], axis=0))
        high, low = halves(jnp.concatenate(turned, axis=1))
        result = dot(self.last[0], high) + dot(self.last[1], high) + dot(self.last[0], low)
        for n in range(2):
            target[pl.ds(2 * i + n, OUTER, stride=MINE), :] = result[
                :, n * WIDE : (n + 1) * WIDE
            ]


def spread(cols, target):
    def body(s, _):
        for q in range(3):
            target[sixteen(3 * s + q), :] = cols[sixteen(s), q * WIDE : (q + 1) * WIDE].astype(F32)
        return 0

    lax.fori_loop(0, N_SEQ, body, 0)


def lanes_at(index):
    return pl.ds(pl.multiple_of(index * WIDE, WIDE), WIDE)


def whole_kernel(*refs):
    (
        layer_hbm, value_hbm, outer_hbm, gate_hbm, conv_hbm, up_hbm, in_shard, out_shard, filter_hbm, taps_hbm,
        *table_hbm,
    ) = refs[:18]
    (
        grad_input, grad_outer, grad_inner, grad_long, grad_short, grad_inproj, grad_outproj,
    ) = refs[18:25]
    (
        layer_input, value_in, outer_gate, gate, conv_output, upstream, filters, *tables,
    ) = refs[25:40]
    (
        whole_out, whole_in, acc, product_t, conv_t, mix_t, conv_rx, mix_rx, mixed_cols, mixed_rx,
        value, value_t, blocks, padded, all_taps, halo, taps_rx, grads, halo_back, short_tx, short_rx,
        conv_f, other_f, out_f, spec_g, spec_h, in_piece, inproj_t, taps_in, taps,
        load_sem, halo_sem, twin_sem, taps_s, taps_r, mix_s, mix_r, conv_s, conv_r,
        back_s, back_r, short_s, short_r, x_s, x_r, p_s,
    ) = refs[40:86]
    rest = refs[86:]
    sems_out, sems_in = rest[:5], rest[5:10]
    scatter_out, scatter_in = rest[10:20], rest[20:30]

    at = place()
    s, y, z, c = at
    ch = lax.axis_index("ch")
    x, low = ch % 4, ch // 4
    twin = {"seq": 4 * ch + s % 4, "ch": s // 4}
    away = s // 4 != ch

    barrier = pltpu.get_barrier_semaphore()
    greet_all(barrier, s)
    for there in (low * 4 + (x + 1) % 4, low * 4 + (x + 3) % 4, (1 - low) * 4 + x):
        pl.semaphore_signal(barrier, inc=1, device_id={"ch": there}, device_id_type=MESH)

    @pl.when(away)
    def _():
        pl.semaphore_signal(barrier, inc=1, device_id=twin, device_id_type=MESH)

    sources = [outer_hbm, conv_hbm, value_hbm, gate_hbm, up_hbm, filter_hbm, layer_hbm, *table_hbm, taps_hbm]
    targets = [outer_gate, conv_output, value_in, gate, upstream, filters, layer_input, *tables, taps_in]
    loads = {}
    for n, (src, dst) in enumerate(zip(sources, targets)):
        copy = pltpu.make_async_copy(src, dst, load_sem.at[n])
        copy.start()
        loads[n] = copy

    def loaded(*which):
        for n in which:
            loads[n].wait()

    @pl.when(away)
    def _():
        pl.semaphore_wait(barrier, N_SEQ - 1 + 4)

    @pl.when(jnp.logical_not(away))
    def _():
        pl.semaphore_wait(barrier, N_SEQ - 1 + 3)

    ring = Gather(out_shard, whole_out, sems_out, at)
    ring.begin()
    edge = remote(
        value_hbm.at[pl.ds(ROWS - 16, 16)],
        halo,
        halo_sem.at[0],
        halo_sem.at[1],
        "seq",
        (s + 1) % N_SEQ,
    )
    edge.start()
    loaded(15)
    spots = own_lanes()
    tap_rows = [
        jnp.sum(taps_in[:, j : j + 1] * spots, axis=0, keepdims=True) for j in range(3)
    ]
    taps[...] = jnp.concatenate(tap_rows + [jnp.zeros((5, WIDE), F32)], axis=0)
    exchange(lambda d: taps, taps_rx.at[s], taps_s, taps_r, s)
    taps_rx[s] = taps[...]
    turn = remote_to(in_shard, in_piece, twin_sem.at[0], twin_sem.at[1], twin)
    stay = pltpu.make_async_copy(in_shard, in_piece, twin_sem.at[2])

    def turn_out():
        @pl.when(away)
        def _():
            turn.start()

        @pl.when(jnp.logical_not(away))
        def _():
            stay.start()

    step = ring.steps()
    loaded(0, 1)
    for r in range(0, ROWS, WIDE):
        rows = pl.ds(r, WIDE)
        product = outer_gate[rows, :].astype(F32) * conv_output[rows, :].astype(F32)
        product_t[:, rows] = product.T.astype(BF16)
    next(step)

    loaded(2, 3)
    for r in range(0, ROWS, WIDE):
        padded[pl.ds(8 + r, WIDE), :] = value_in[pl.ds(r, WIDE), :].astype(F32)
    arrived(lambda d: taps_rx.at[d], taps_s, taps_r, s)
    for g in range(4):
        tile = taps_rx[8 * g]
        for i in range(1, 8):
            tile = tile + taps_rx[8 * g + i]
        all_taps[:, pl.ds(g * WIDE, WIDE)] = tile
    edge.wait_recv()
    padded[pl.ds(0, 8), :] = jnp.where(s == 0, 0.0, halo[...].astype(F32)[8:, :])
    next(step)

    def smooth_rows(r):
        smooth = all_taps[pl.ds(0, 1), :] * padded[pl.ds(8 + r, WIDE), :]
        for j in range(1, 3):
            smooth = smooth + all_taps[pl.ds(j, 1), :] * padded[pl.ds(8 + r - j, WIDE), :]
        return smooth

    for r in range(0, ROWS, WIDE):
        mixed = gate[pl.ds(r, WIDE), :].astype(F32) * smooth_rows(r)
        mix_t[:, pl.ds(r, WIDE)] = mixed.T.astype(BF16)
    outs = Scatter(scatter_out, at)
    next(step)

    def multiply(sub, o, first=False):
        m = ring.ready(sub, o)
        cols = pl.ds(pl.multiple_of(m * 2 * WIDE, 2 * WIDE), 2 * WIDE)
        shards = jnp.concatenate([whole_out[2 * m], whole_out[2 * m + 1]], axis=1)
        part = lax.dot_general(
            upstream[:, cols], shards, (((1,), (1,)), ((), ())), preferred_element_type=F32
        )
        acc[...] = part if first else acc[...] + part

    loaded(4)
    multiply(0, 0, True)
    multiply(0, 1)
    multiply(0, -1)
    outs.partials(product_t, upstream, 0, 1)
    order = ((1, (0,)), (0, (2, -2)), (1, (1, -1)), (0, (3, -3)), (1, (2, -2)), (0, (4,)))
    for n, (sub, offsets) in enumerate(order):
        next(step)
        if n == 1:
            turn_out()
        for o in offsets:
            multiply(sub, o)
        if n < 5:
            outs.partials(product_t, upstream, n + 1, n + 2)
    multiply(1, 3)
    multiply(1, -3)
    for _ in step:
        pass
    multiply(1, 4)

    for r in range(0, ROWS, WIDE):
        rows = pl.ds(r, WIDE)
        conv = acc[rows, :] * outer_gate[rows, :].astype(F32)
        conv_t[:, rows] = conv.T.astype(BF16)
    exchange(lambda d: conv_t.at[sixteen(d)], conv_rx.at[sixteen(s)], conv_s, conv_r, s)
    conv_rx[sixteen(s), :] = conv_t[sixteen(s), :]

    @pl.when(away)
    def _():
        turn.wait_recv()

    @pl.when(jnp.logical_not(away))
    def _():
        stay.wait()

    ring_in = Gather(in_piece, whole_in, sems_in, at)
    ring_in.begin()
    in_step = ring_in.steps()
    for r in range(0, ROWS, WIDE):
        rows = pl.ds(r, WIDE)
        grad_outer[rows, :] = (acc[rows, :] * conv_output[rows, :].astype(F32)).astype(BF16)
    loaded(5, *range(7, 15))

    def filter_rows(j, _):
        other_f[sixteen(j), :] = filters[:, lanes_at(j)].astype(F32)
        return 0

    lax.fori_loop(0, OUTER, filter_rows, 0)
    spectra = Spectra(tables)

    def take_filter(i, _):
        spec_h[i] = spectra.forward(other_f, i)
        return 0

    lax.fori_loop(0, 4, take_filter, 0)
    next(in_step)
    lax.fori_loop(4, 8, take_filter, 0)
    outs.partials(product_t, upstream, 6, 8)
    out_step = outs.steps()
    next(out_step)
    next(in_step)

    arrived(lambda d: conv_rx.at[sixteen(d)], conv_s, conv_r, s)
    exchange(lambda d: mix_t.at[sixteen(d)], mix_rx.at[sixteen(s)], mix_s, mix_r, s)
    mix_rx[sixteen(s), :] = mix_t[sixteen(s), :]
    spread(conv_rx, conv_f)

    def take_mixed(i, _):
        spec = spectra.forward(conv_f, i)
        spec_g[i] = spec
        spectra.inverse(spec, spec_h[i], out_f, i)
        return 0

    lax.fori_loop(0, 3, take_mixed, 0)
    next(in_step)
    lax.fori_loop(3, 6, take_mixed, 0)
    next(in_step)
    lax.fori_loop(6, 8, take_mixed, 0)

    def gather_rows(n, _):
        for q in range(3):
            mixed_cols[sixteen(n), q * WIDE : (q + 1) * WIDE] = out_f[
                sixteen(3 * n + q), :
            ].astype(BF16)
        return 0

    lax.fori_loop(0, N_SEQ, gather_rows, 0)
    exchange(lambda d: mixed_cols.at[sixteen(d)], mixed_rx.at[sixteen(s)], back_s, back_r, s)
    mixed_rx[sixteen(s), :] = mixed_cols[sixteen(s), :]

    def take_long(i, _):
        spectra.inverse(spec_g[i], spectra.forward(other_f, i), out_f, i)
        return 0

    next(in_step)
    arrived(lambda d: mix_rx.at[sixteen(d)], mix_s, mix_r, s)
    spread(mix_rx, other_f)
    lax.fori_loop(0, 3, take_long, 0)
    next(in_step)
    lax.fori_loop(3, 6, take_long, 0)
    next(in_step)
    arrived(lambda d: mixed_rx.at[sixteen(d)], back_s, back_r, s)
    next(out_step)
    next(out_step)

    edge_back = remote(
        grads.at[pl.ds(0, 8)],
        halo_back,
        halo_sem.at[2],
        halo_sem.at[3],
        "seq",
        (s + N_SEQ - 1) % N_SEQ,
    )
    for r in range(0, ROWS, WIDE):
        rows = pl.ds(r, WIDE)
        mixed = mixed_rx[:, rows].astype(F32).T
        grads[rows, :] = mixed * gate[rows, :].astype(F32)
        if r == 0:
            edge_back.start()
        grad_inner[rows, :] = (mixed * smooth_rows(r)).astype(BF16)
    edge_back.wait_recv()
    grads[pl.ds(ROWS, 8), :] = jnp.where(s == N_SEQ - 1, 0.0, halo_back[...])
    for r in range(0, ROWS, WIDE):
        rows = pl.ds(r, WIDE)
        out = all_taps[pl.ds(0, 1), :] * grads[rows, :]
        for j in range(1, 3):
            out = out + all_taps[pl.ds(j, 1), :] * grads[pl.ds(r + j, WIDE), :]
        value[rows, :] = out.astype(BF16)
        value_t[:, rows] = out.T.astype(BF16)

    def block(sub, o):
        return (1 - low if sub else low) * 4 + (x + o + 4) % 4

    def x_hop(di, d, sub):
        o = -SIGNS[di] * (d - 1)
        return remote(
            value if (sub, o) == (0, 0) else blocks.at[block(sub, o)],
            blocks.at[block(sub, o)],
            x_s.at[di, d - 1, sub],
            x_r.at[di, d - 1, sub],
            "ch",
            low * 4 + (x + SIGNS[di] + 4) % 4,
        )

    def x_wait(di, d, sub):
        here = blocks.at[block(sub, -SIGNS[di] * d)]
        remote(
            here, here, x_s.at[di, d - 1, sub], x_r.at[di, d - 1, sub], "ch", ch
        ).wait_recv()

    partner = remote(
        value, blocks.at[block(0, 0)], p_s.at[0], p_s.at[1], "ch", (1 - low) * 4 + x
    )
    hops = []

    def x_go(di, d, sub):
        hop = x_hop(di, d, sub)
        hop.start()
        hops.append(hop)

    x_go(0, 1, 0)
    x_go(1, 1, 0)
    partner.start()
    next(out_step)
    blocks[block(0, 0)] = value[...]
    loaded(6)
    total = Scatter(scatter_in, at)
    total.partials(value_t, layer_input, 0, 3)
    step = total.steps()
    next(step)
    total.partials(value_t, layer_input, 3, 6)
    next(step)
    next(out_step)
    total.partials(value_t, layer_input, 6, 8)
    next(step)
    partner.wait_recv()
    x_go(0, 1, 1)
    x_go(1, 1, 1)
    next(step)
    next(out_step)

    sums = []
    for j in range(3):
        part = jnp.zeros((1, CHANS), F32)
        for r in range(0, ROWS, WIDE):
            part = part + jnp.sum(
                grads[pl.ds(r, WIDE), :] * padded[pl.ds(8 + r - j, WIDE), :], axis=0, keepdims=True
            )
        sums.append(part)
    short_tx[...] = jnp.concatenate(sums + [jnp.zeros((5, CHANS), F32)], axis=0)
    exchange(lambda d: short_tx.at[:, lanes_at(d // 8)], short_rx.at[s], short_s, short_r, s)
    short_rx[s] = short_tx[:, lanes_at(s // 8)]

    x_wait(0, 1, 0)
    x_go(0, 2, 0)
    x_wait(1, 1, 0)
    next(step)
    next(out_step)
    next(in_step)
    next(step)
    next(out_step)
    next(in_step)
    x_wait(1, 1, 1)
    x_go(1, 2, 1)
    next(step)
    for _ in out_step:
        pass
    for _ in in_step:
        pass
    lax.fori_loop(6, 8, take_long, 0)
    next(step)

    def long_rows(j, _):
        grad_long[:, lanes_at(j)] = out_f[sixteen(j), :]
        return 0

    lax.fori_loop(0, OUTER, long_rows, 0)
    for sub in range(2):
        for o in range(-3, 5):
            ring_in.ready(sub, o)

    def finish(n, first=False):
        w = jnp.concatenate([whole_in[4 * n + i] for i in range(4)], axis=0)
        part = lax.dot_general(
            blocks[n], w, (((1,), (1,)), ((), ())), preferred_element_type=F32
        )
        acc[...] = part if first else acc[...] + part

    finish(ch, True)
    finish(block(1, 0))
    finish(block(0, -1))
    finish(block(0, 1))
    finish(block(1, 1))
    for _ in step:
        pass
    outs.finish(grad_outproj)
    x_wait(0, 1, 1)
    finish(block(1, -1))
    total.finish(inproj_t)
    grad_inproj[...] = inproj_t[...].T
    arrived(lambda d: short_rx.at[d], short_s, short_r, s)
    tile = short_rx[0]
    for i in range(1, N_SEQ):
        tile = tile + short_rx[i]
    grad_short[...] = tile
    x_wait(0, 2, 0)
    finish(block(0, 2))
    x_wait(1, 2, 1)
    finish(block(1, 2))
    grad_input[...] = acc[...].astype(BF16)
    edge_back.wait_send()

    for hop in hops:
        hop.wait_send()
    partner.wait_send()
    edge.wait_send()
    ring.end()
    ring_in.end()

    @pl.when(away)
    def _():
        turn.wait_send()


    left(taps, taps_s, taps_r, s)
    left(mix_t.at[sixteen(0)], mix_s, mix_r, s)
    left(conv_t.at[sixteen(0)], conv_s, conv_r, s)
    left(mixed_cols.at[sixteen(0)], back_s, back_r, s)
    left(short_rx.at[0], short_s, short_r, s)


TAPS_AT = 4


def own_lanes():
    lane = (lax.axis_index("seq") % 8) * MINE
    rows = lax.broadcasted_iota(jnp.int32, (MINE, WIDE), 0)
    cols = lax.broadcasted_iota(jnp.int32, (MINE, WIDE), 1)
    return jnp.where(cols == rows + lane, 1.0, 0.0).astype(F32)


def hand_out(*refs):
    *refs, tile, sems = refs
    n = len(refs) // 3
    inward = [
        pltpu.make_async_copy(refs[i], tile if i == TAPS_AT else refs[2 * n + i], sems.at[i])
        for i in range(n)
    ]
    outward = [
        pltpu.make_async_copy(refs[2 * n + i], refs[n + i], sems.at[n + i]) for i in range(n)
    ]
    for copy in inward:
        copy.start()
    for i in range(n):
        inward[i].wait()
        if i != TAPS_AT:
            outward[i].start()
    refs[2 * n + TAPS_AT][...] = lax.dot_general(
        own_lanes(),
        tile[...],
        (((1,), (1,)), ((), ())),
        precision=lax.Precision.HIGHEST,
        preferred_element_type=F32,
    )[:, :3]
    outward[TAPS_AT].start()
    for copy in outward:
        copy.wait()


def shards(
    layer_input, value_proj, outer_gate, inner_gate, conv_output,
    upstream, in_weight, out_weight, long_filter, short_filter,
):
    dma = pltpu.SemaphoreType.DMA
    peers = dma((N_SEQ,))
    vmem = pltpu.VMEM
    tables = [jnp.asarray(t) for t in dft_tables()]
    outs = [
        jax.ShapeDtypeStruct(shape, dtype)
        for shape, dtype in (
            ((ROWS, CHANS), BF16),
            ((ROWS, CHANS), BF16),
            ((ROWS, CHANS), BF16),
            ((MINE, LENGTH), F32),
            ((8, WIDE), F32),
            ((WIDE, CHANS), F32),
            ((CHANS, WIDE), F32),
        )
    ]
    args = (
        layer_input, value_proj, outer_gate, inner_gate, conv_output, upstream, in_weight, out_weight,
        long_filter[0], short_filter[0], *tables,
    )
    local = [vmem((ROWS, CHANS), BF16)] * 4
    block = vmem((CHANS, ROWS), BF16)
    signal = vmem((MINE * OUTER, WIDE), F32)
    spectrum = vmem((MINE // 2, 2 * OUTER, 2 * WIDE), F32)
    scratch = [
        vmem((ROWS, DEEP), BF16),
        *local,
        vmem((ROWS, DEEP), BF16),
        vmem((MINE, LENGTH), BF16),
        *[vmem(t.shape, t.dtype) for t in tables],
        vmem((N_SEQ, CHANS, WIDE), BF16),
        vmem((N_SEQ, WIDE, CHANS), BF16),
        vmem((ROWS, CHANS), F32),
        *[block] * 7,
        vmem((ROWS, CHANS), BF16),
        block,
        vmem((8, ROWS, CHANS), BF16),
        vmem((ROWS + 8, CHANS), F32),
        vmem((8, CHANS), F32),
        vmem((16, CHANS), BF16),
        vmem((N_SEQ, 8, WIDE), F32),
        vmem((ROWS + 8, CHANS), F32),
        vmem((8, CHANS), F32),
        vmem((8, CHANS), F32),
        vmem((N_SEQ, 8, WIDE), F32),
        signal, signal, signal, spectrum, spectrum,
        vmem((WIDE, CHANS), BF16),
        vmem((CHANS, WIDE), F32),
        vmem((MINE, 3), F32), vmem((8, WIDE), F32),
        dma((16,)), dma((4,)), dma((3,)),
        *[peers] * 10,
        dma((2, 2, 2)), dma((2, 2, 2)), dma((2,)),
        *Gather.sems, *Gather.sems, *Scatter.scratch(), *Scatter.scratch(),
    ]
    given = list(outs)
    given[TAPS_AT] = jax.ShapeDtypeStruct((MINE, 3), F32)
    results = pl.pallas_call(
        whole_kernel,
        out_shape=outs,
        in_specs=[pl.BlockSpec(memory_space=pl.ANY)] * len(args),
        out_specs=[pl.BlockSpec(memory_space=pltpu.VMEM)] * len(outs),
        scratch_shapes=scratch,
        compiler_params=pltpu.CompilerParams(
            collective_id=0, has_side_effects=True, vmem_limit_bytes=60 * 2**20
        ),
        cost_estimate=pl.CostEstimate(
            flops=12 * 10**9, bytes_accessed=20 * 2**20, transcendentals=0
        ),
    )(*args)
    (
        grad_input, grad_outer, grad_inner, grad_long, grad_short, grad_inproj, grad_outproj,
    ) = pl.pallas_call(
        hand_out,
        out_shape=given,
        in_specs=[pl.BlockSpec(memory_space=pl.ANY)] * len(outs),
        out_specs=[pl.BlockSpec(memory_space=pl.ANY)] * len(outs),
        scratch_shapes=[
            *[vmem(o.shape, o.dtype) for o in given],
            vmem((8, WIDE), F32),
            dma((2 * len(outs),)),
        ],
    )(*results)
    return (
        grad_input,
        grad_outer,
        grad_inner,
        grad_long[None],
        grad_short[None],
        grad_inproj,
        grad_outproj,
    )


def solution(mesh):
    in_specs = (
        P("seq", None),
        P("seq", "ch"),
        P("seq", "ch"),
        P("seq", "ch"),
        P("seq", "ch"),
        P("seq", None),
        P("seq", "ch"),
        P("ch", "seq"),
        P("ch", "seq", None),
        P("ch", "seq", None),
    )
    out_specs = (
        P("seq", "ch"),
        P("seq", "ch"),
        P("seq", "ch"),
        P("ch", "seq", None),
        P("ch", "seq", None),
        P("seq", "ch"),
        P("ch", "seq"),
    )
    return jax.shard_map(shards, mesh=mesh, in_specs=in_specs, out_specs=out_specs, check_vma=False)
```

```python
import math

import ml_dtypes
import numpy as np
import jax
import jax.numpy as jnp
from jax import lax
from jax.experimental import pallas as pl
from jax.experimental.pallas import tpu as pltpu
from jax.sharding import PartitionSpec as P

MESH = pl.DeviceIdType.MESH
F32 = jnp.float32
BF16 = jnp.bfloat16
N_SEQ = 32
ROWS = 384
CHANS = 512
MINE = 16
WIDE = 128
DEEP = 4096
LENGTH = N_SEQ * ROWS
OUTER = LENGTH // WIDE
SIGNS = (1, -1)


def split_table(table):
    high = table.astype(ml_dtypes.bfloat16)
    low = (table - high.astype(np.float64)).astype(ml_dtypes.bfloat16)
    return high, low


def dft_tables():
    a = np.arange(OUTER)
    b = np.arange(WIDE)
    k1 = np.arange(OUTER)
    k2 = np.arange(WIDE)
    turn = np.pi / (2 * LENGTH)
    outer = 2 * np.pi * np.outer(k1, a) / OUTER + turn * WIDE * a[None, :]
    twist = 2 * np.pi * np.outer(k1, b) / LENGTH + turn * b[None, :]
    inner = 2 * np.pi * np.outer(b, k2) / WIDE
    first = np.concatenate([np.cos(outer), -np.sin(outer)], axis=0)
    co, si = np.cos(inner), np.sin(inner)
    second = np.block([[co, -si], [si, co]])
    third = np.block([[co, si], [-si, co]])
    last = np.concatenate([np.cos(outer).T, -np.sin(outer).T], axis=1) / LENGTH
    first_h, first_l = split_table(first)
    second_h, second_l = split_table(second)
    third_h, third_l = split_table(third)
    last_h, last_l = split_table(last)
    return (
        np.concatenate([first_h, first_l], axis=0),
        second_h,
        second_l,
        third_h,
        third_l,
        np.stack([last_h, last_l]),
        np.cos(twist).astype(np.float32),
        np.sin(twist).astype(np.float32),
    )


def remote_to(src, dst, send, recv, device):
    return pltpu.make_async_remote_copy(
        src_ref=src,
        dst_ref=dst,
        send_sem=send,
        recv_sem=recv,
        device_id=device,
        device_id_type=MESH,
    )


def remote(src, dst, send, recv, axis, index):
    return remote_to(src, dst, send, recv, {axis: index})


def place():
    s = lax.axis_index("seq")
    return s, s // 16, (s // 2) % 8, s % 2


def at_seq(y, z, c):
    return y * 16 + z * 2 + c


def greet_all(barrier, s):
    def body(i, _):
        pl.semaphore_signal(
            barrier, inc=1, device_id={"seq": (s + i) % N_SEQ}, device_id_type=MESH
        )
        return 0

    lax.fori_loop(1, N_SEQ, body, 0)


def exchange(source_of, target, sends, recvs, s):
    def body(i, _):
        dst = (s + i) % N_SEQ
        remote(source_of(dst), target, sends.at[i], recvs.at[i], "seq", dst).start()
        return 0

    lax.fori_loop(1, N_SEQ, body, 0)


def arrived(landing_of, sends, recvs, s):
    def body(i, _):
        src = (s + N_SEQ - i) % N_SEQ
        here = landing_of(src)
        remote(here, here, sends.at[i], recvs.at[i], "seq", src).wait_recv()
        return 0

    lax.fori_loop(1, N_SEQ, body, 0)


def left(piece, sends, recvs, s):
    def body(i, _):
        remote(piece, piece, sends.at[i], recvs.at[i], "seq", (s + i) % N_SEQ).wait_send()
        return 0

    lax.fori_loop(1, N_SEQ, body, 0)


OVER_Y = (0, 3, 5, 4)
EARLY_Y = (0, 1, 7, 4)


class Gather:
    sems = [
        pltpu.SemaphoreType.DMA((2, 4, 2)),
        pltpu.SemaphoreType.DMA((2, 4, 2)),
        pltpu.SemaphoreType.DMA((2, 8)),
        pltpu.SemaphoreType.DMA((2, 8)),
        pltpu.SemaphoreType.DMA((9,)),
    ]

    def __init__(self, shard, whole, sems, at):
        self.shard, self.whole, self.at = shard, whole, at
        self.half = shard.shape[0] // 2
        self.zs, self.zr, self.cs, self.cr, self.ys = sems
        self.started = []

    def slot(self, sub, o, other=False):
        _, y, z, c = self.at
        yy = 1 - y if sub else y
        return at_seq(yy, (z + o + 8) % 8, 1 - c if other else c)

    def go(self, copy):
        copy.start()
        self.started.append(copy)

    def source(self, sub, o):
        if sub == 0 and o == 0:
            return self.shard
        return self.whole.at[self.slot(sub, o)]

    def hop(self, di, d, sub):
        _, y, z, c = self.at
        o = -SIGNS[di] * (d - 1)
        src, dst = self.source(sub, o), self.whole.at[self.slot(sub, o)]
        if d == 4:
            rows = pl.ds(di * self.half, self.half)
            src = dst = self.whole.at[self.slot(sub, o), rows]
        self.go(
            remote(
                src,
                dst,
                self.zs.at[di, d - 1, sub],
                self.zr.at[di, d - 1, sub],
                "seq",
                at_seq(y, (z + SIGNS[di] + 8) % 8, c),
            )
        )

    def landed(self, di, d, sub):
        here = self.whole.at[self.slot(sub, -SIGNS[di] * d)]
        if d == 4:
            here = self.whole.at[self.slot(sub, 4), pl.ds(di * self.half, self.half)]
        remote(
            here, here, self.zs.at[di, d - 1, sub], self.zr.at[di, d - 1, sub], "seq", self.at[0]
        ).wait_recv()

    def share(self, sub, o):
        _, y, z, c = self.at
        self.go(
            remote(
                self.source(sub, o),
                self.whole.at[self.slot(sub, o)],
                self.cs.at[sub, o % 8],
                self.cr.at[sub, o % 8],
                "seq",
                at_seq(y, z, 1 - c),
            )
        )

    def over_y(self, n):
        _, y, z, c = self.at
        self.go(
            remote(
                self.source(0, EARLY_Y[n]),
                self.whole.at[self.slot(0, EARLY_Y[n])],
                self.ys.at[2 * n],
                self.ys.at[2 * n + 1],
                "seq",
                at_seq(1 - y, z, c),
            )
        )

    def from_y(self, n):
        here = self.whole.at[self.slot(1, EARLY_Y[n])]
        remote(
            here, here, self.ys.at[2 * n], self.ys.at[2 * n + 1], "seq", self.at[0]
        ).wait_recv()
        self.share(1, EARLY_Y[n])

    def begin(self):
        self.hop(0, 1, 0)
        self.hop(1, 1, 0)
        self.over_y(0)
        self.share(0, 0)
        self.keep = pltpu.make_async_copy(
            self.shard, self.whole.at[self.slot(0, 0)], self.ys.at[8]
        )
        self.keep.start()

    def serve(self, d, sub, on):
        for di in range(2):
            self.landed(di, d, sub)
            if on:
                self.hop(di, d + 1, sub)
        for di in range(2):
            if d < 4:
                self.share(sub, -SIGNS[di] * d)

    def steps(self):
        self.serve(1, 0, True)
        self.over_y(1)
        self.over_y(2)
        yield
        self.from_y(0)
        yield
        self.serve(2, 0, True)
        yield
        self.from_y(1)
        self.hop(1, 2, 1)
        self.from_y(2)
        self.hop(0, 2, 1)
        yield
        self.serve(3, 0, True)
        yield
        self.serve(2, 1, True)
        yield
        self.serve(4, 0, False)
        self.over_y(3)
        self.share(0, 4)
        yield
        self.serve(3, 1, False)
        yield
        self.from_y(3)
        yield

    def ready(self, sub, o):
        _, y, z, c = self.at
        if (sub, o) == (0, 0):
            self.keep.wait()
        here = self.whole.at[self.slot(sub, o, other=True)]
        remote(
            here, here, self.cs.at[sub, o % 8], self.cr.at[sub, o % 8], "seq", self.at[0]
        ).wait_recv()
        yy = 1 - y if sub else y
        return yy * 8 + (z + o + 8) % 8

    def end(self):
        for copy in self.started:
            copy.wait_send()


class Scatter:
    @staticmethod
    def scratch():
        return [
            pltpu.VMEM((2, 8, CHANS, WIDE), BF16),
            pltpu.VMEM((2, 8, CHANS, WIDE), BF16),
            pltpu.VMEM((2, 8, CHANS, WIDE), BF16),
            pltpu.VMEM((2, 4, 2, CHANS, WIDE), BF16),
            pltpu.VMEM((4, CHANS, WIDE), BF16),
            pltpu.SemaphoreType.DMA((2, 4, 2)),
            pltpu.SemaphoreType.DMA((2, 4, 2)),
            pltpu.SemaphoreType.DMA((2, 8)),
            pltpu.SemaphoreType.DMA((2, 8)),
            pltpu.SemaphoreType.DMA((8,)),
        ]

    def __init__(self, scratch, at):
        self.at = at
        self.own, self.tx, self.rx, self.zrx, self.yrx = scratch[:5]
        self.zs, self.zr, self.cs, self.cr, self.ys = scratch[5:]
        self.started = []

    def go(self, copy):
        copy.start()
        self.started.append(copy)

    def hand(self, sub, o):
        _, y, z, c = self.at
        return remote(
            self.tx.at[sub, o],
            self.rx.at[sub, o],
            self.cs.at[sub, o],
            self.cr.at[sub, o],
            "seq",
            at_seq(y, z, 1 - c),
        )

    def partials(self, left_t, right, first=0, last=8):
        _, y, z, c = self.at

        def body(i, _):
            o = (4 + (1 - 2 * (i % 2)) * ((i + 1) // 2) + 8) % 8
            columns = []
            for sub in range(2):
                m = (1 - y if sub else y) * 8 + (z + o) % 8
                columns.append(right[:, pl.ds(pl.multiple_of(m * 2 * WIDE, 2 * WIDE), 2 * WIDE)])
            both = jnp.dot(
                left_t[...], jnp.concatenate(columns, axis=1), preferred_element_type=F32
            )
            for sub in range(2):
                low = both[:, 2 * sub * WIDE : (2 * sub + 1) * WIDE].astype(BF16)
                high = both[:, (2 * sub + 1) * WIDE : (2 * sub + 2) * WIDE].astype(BF16)
                self.tx[sub, o] = jnp.where(c == 0, high, low)
                self.hand(sub, o).start()
                self.own[sub, o] = jnp.where(c == 0, low, high)
            return 0

        lax.fori_loop(first, last, body, 0)

    def hop(self, di, d, sub):
        _, y, z, c = self.at
        o = (SIGNS[di] * d) % 8
        src, dst = self.own.at[sub, o], self.zrx.at[di, d - 1, sub]
        if d == 4:
            half = CHANS // 2
            src = self.own.at[sub, o, pl.ds(di * half, half)]
            dst = self.zrx.at[di, d - 1, sub, pl.ds(0, half)]
        return remote(
            src,
            dst,
            self.zs.at[di, d - 1, sub],
            self.zr.at[di, d - 1, sub],
            "seq",
            at_seq(y, (z + SIGNS[di] + 8) % 8, c),
        )

    def over_y(self, n):
        _, y, z, c = self.at
        return remote(
            self.own.at[1, OVER_Y[n]],
            self.yrx.at[n],
            self.ys.at[2 * n],
            self.ys.at[2 * n + 1],
            "seq",
            at_seq(1 - y, z, c),
        )

    def both(self, sub, o):
        self.hand(sub, o).wait_recv()
        return self.own[sub, o].astype(F32) + self.rx[sub, o].astype(F32)

    def with_y(self, n):
        total = self.both(0, OVER_Y[n])
        self.over_y(n).wait_recv()
        return total + self.yrx[n].astype(F32)

    def steps(self):
        for n in (3, 1, 2):
            o = OVER_Y[n]
            self.own[1, o] = self.both(1, o).astype(BF16)
            self.go(self.over_y(n))
        yield
        self.own[0, 4] = self.with_y(3).astype(BF16)
        self.go(self.hop(0, 4, 0))
        self.go(self.hop(1, 4, 0))
        yield
        half = CHANS // 2
        for d, sub in ((2, 1), (3, 0), (1, 1), (2, 0), (0, 1), (1, 0)):
            if d == 0:
                self.own[1, 0] = self.ended(1).astype(BF16)
                self.go(self.over_y(0))
                yield
                continue
            for di in range(2):
                o = (SIGNS[di] * d) % 8
                if d == 3:
                    total = self.with_y(1 + di)
                    self.hop(di, 4, 0).wait_recv()
                    parts = [total[:half], total[half:]]
                    parts[di] = parts[di] + self.zrx[di, 3, 0, :half].astype(F32)
                    total = jnp.concatenate(parts, axis=0)
                else:
                    total = self.both(sub, o)
                    if (d, sub) != (2, 1):
                        self.hop(di, d + 1, sub).wait_recv()
                        total = total + self.zrx[di, d, sub].astype(F32)
                self.own[sub, o] = total.astype(BF16)
                self.go(self.hop(di, d, sub))
            yield

    def ended(self, sub):
        value = self.both(sub, 0)
        for di in range(2):
            self.hop(di, 1, sub).wait_recv()
            value = value + self.zrx[di, 0, sub].astype(F32)
        return value

    def finish(self, out):
        out[...] = self.ended(0)
        self.over_y(0).wait_recv()
        out[...] += self.yrx[0].astype(F32)
        for copy in self.started:
            copy.wait_send()

        def body(i, _):
            for sub in range(2):
                self.hand(sub, i).wait_send()
            return 0

        lax.fori_loop(0, 8, body, 0)


def sixteen(index):
    return pl.ds(pl.multiple_of(index * MINE, MINE), MINE)


def halves(x):
    high = x.astype(BF16)
    return high, (x - high.astype(F32)).astype(BF16)


def dot(a, b):
    return jnp.dot(a, b, preferred_element_type=F32)


def dot_three(x, table_h, table_l):
    high, low = halves(x)
    return dot(high, table_h[...]) + dot(high, table_l[...]) + dot(low, table_h[...])


class Spectra:
    def __init__(self, tables):
        (
            self.first,
            self.second_h,
            self.second_l,
            self.third_h,
            self.third_l,
            self.last,
            self.cos_t,
            self.sin_t,
        ) = tables

    def forward(self, source, i):
        signals = jnp.concatenate(
            [source[pl.ds(2 * i + n, OUTER, stride=MINE), :] for n in range(2)], axis=1
        ).astype(BF16)
        both = dot(self.first[...], signals)
        both = both[: 2 * OUTER] + both[2 * OUTER :]
        cos, sin = self.cos_t[...], self.sin_t[...]
        rows = []
        for n in range(2):
            re = both[:OUTER, n * WIDE : (n + 1) * WIDE]
            im = both[OUTER:, n * WIDE : (n + 1) * WIDE]
            rows.append(jnp.concatenate([re * cos + im * sin, im * cos - re * sin], axis=1))
        return dot_three(jnp.concatenate(rows, axis=0), self.second_h, self.second_l)

    def inverse(self, later, earlier, target, i):
        a, b = later[:, :WIDE], later[:, WIDE:]
        c, d = earlier[:, :WIDE], earlier[:, WIDE:]
        spec = jnp.concatenate([a * c + b * d, b * c - a * d], axis=1)
        mid = dot_three(spec, self.third_h, self.third_l)
        cos, sin = self.cos_t[...], self.sin_t[...]
        turned = []
        for n in range(2):
            re = mid[n * OUTER : (n + 1) * OUTER, :WIDE]
            im = mid[n * OUTER : (n + 1) * OUTER, WIDE:]
            turned.append(jnp.concatenate([re * cos - im * sin, im * cos + re * sin], axis=0))
        high, low = halves(jnp.concatenate(turned, axis=1))
        result = dot(self.last[0], high) + dot(self.last[1], high) + dot(self.last[0], low)
        for n in range(2):
            target[pl.ds(2 * i + n, OUTER, stride=MINE), :] = result[
                :, n * WIDE : (n + 1) * WIDE
            ]


def spread(cols, target):
    def body(s, _):
        for q in range(3):
            target[sixteen(3 * s + q), :] = cols[sixteen(s), q * WIDE : (q + 1) * WIDE].astype(F32)
        return 0

    lax.fori_loop(0, N_SEQ, body, 0)


def lanes_at(index):
    return pl.ds(pl.multiple_of(index * WIDE, WIDE), WIDE)


def whole_kernel(*refs):
    (
        layer_hbm, value_hbm, outer_hbm, gate_hbm, conv_hbm, up_hbm, in_shard, out_shard, filter_hbm, taps_hbm,
        *table_hbm,
    ) = refs[:18]
    (
        grad_input, grad_outer, grad_inner, grad_long, grad_short, grad_inproj, grad_outproj,
    ) = refs[18:25]
    (
        layer_input, value_in, outer_gate, gate, conv_output, upstream, filters, *tables,
    ) = refs[25:40]
    (
        whole_out, whole_in, acc, product_t, conv_t, mix_t, conv_rx, mix_rx, mixed_cols, mixed_rx,
        value, value_t, blocks, padded, all_taps, halo, taps_rx, grads, halo_back, short_tx, short_rx,
        conv_f, other_f, out_f, spec_g, spec_h, in_piece, inproj_t, taps_in, taps,
        load_sem, halo_sem, twin_sem, taps_s, taps_r, mix_s, mix_r, conv_s, conv_r,
        back_s, back_r, short_s, short_r, x_s, x_r, p_s,
    ) = refs[40:86]
    rest = refs[86:]
    sems_out, sems_in = rest[:5], rest[5:10]
    scatter_out, scatter_in = rest[10:20], rest[20:30]

    at = place()
    s, y, z, c = at
    ch = lax.axis_index("ch")
    x, low = ch % 4, ch // 4
    twin = {"seq": 4 * ch + s % 4, "ch": s // 4}
    away = s // 4 != ch

    barrier = pltpu.get_barrier_semaphore()
    greet_all(barrier, s)
    for there in (low * 4 + (x + 1) % 4, low * 4 + (x + 3) % 4, (1 - low) * 4 + x):
        pl.semaphore_signal(barrier, inc=1, device_id={"ch": there}, device_id_type=MESH)

    @pl.when(away)
    def _():
        pl.semaphore_signal(barrier, inc=1, device_id=twin, device_id_type=MESH)

    sources = [outer_hbm, conv_hbm, value_hbm, gate_hbm, up_hbm, filter_hbm, layer_hbm, *table_hbm, taps_hbm]
    targets = [outer_gate, conv_output, value_in, gate, upstream, filters, layer_input, *tables, taps_in]
    loads = {}
    for n, (src, dst) in enumerate(zip(sources, targets)):
        copy = pltpu.make_async_copy(src, dst, load_sem.at[n])
        copy.start()
        loads[n] = copy

    def loaded(*which):
        for n in which:
            loads[n].wait()

    @pl.when(away)
    def _():
        pl.semaphore_wait(barrier, N_SEQ - 1 + 4)

    @pl.when(jnp.logical_not(away))
    def _():
        pl.semaphore_wait(barrier, N_SEQ - 1 + 3)

    ring = Gather(out_shard, whole_out, sems_out, at)
    ring.begin()
    edge = remote(
        value_hbm.at[pl.ds(ROWS - 16, 16)],
        halo,
        halo_sem.at[0],
        halo_sem.at[1],
        "seq",
        (s + 1) % N_SEQ,
    )
    edge.start()
    loaded(15)
    spots = own_lanes()
    tap_rows = [
        jnp.sum(taps_in[:, j : j + 1] * spots, axis=0, keepdims=True) for j in range(3)
    ]
    taps[...] = jnp.concatenate(tap_rows + [jnp.zeros((5, WIDE), F32)], axis=0)
    exchange(lambda d: taps, taps_rx.at[s], taps_s, taps_r, s)
    taps_rx[s] = taps[...]
    turn = remote_to(in_shard, in_piece, twin_sem.at[0], twin_sem.at[1], twin)
    stay = pltpu.make_async_copy(in_shard, in_piece, twin_sem.at[2])

    def turn_out():
        @pl.when(away)
        def _():
            turn.start()

        @pl.when(jnp.logical_not(away))
        def _():
            stay.start()

    step = ring.steps()
    loaded(0, 1)
    for r in range(0, ROWS, WIDE):
        rows = pl.ds(r, WIDE)
        product = outer_gate[rows, :].astype(F32) * conv_output[rows, :].astype(F32)
        product_t[:, rows] = product.T.astype(BF16)
    next(step)

    loaded(2, 3)
    for r in range(0, ROWS, WIDE):
        padded[pl.ds(8 + r, WIDE), :] = value_in[pl.ds(r, WIDE), :].astype(F32)
    arrived(lambda d: taps_rx.at[d], taps_s, taps_r, s)
    for g in range(4):
        tile = taps_rx[8 * g]
        for i in range(1, 8):
            tile = tile + taps_rx[8 * g + i]
        all_taps[:, pl.ds(g * WIDE, WIDE)] = tile
    edge.wait_recv()
    padded[pl.ds(0, 8), :] = jnp.where(s == 0, 0.0, halo[...].astype(F32)[8:, :])
    next(step)

    def smooth_rows(r):
        smooth = all_taps[pl.ds(0, 1), :] * padded[pl.ds(8 + r, WIDE), :]
        for j in range(1, 3):
            smooth = smooth + all_taps[pl.ds(j, 1), :] * padded[pl.ds(8 + r - j, WIDE), :]
        return smooth

    for r in range(0, ROWS, WIDE):
        mixed = gate[pl.ds(r, WIDE), :].astype(F32) * smooth_rows(r)
        mix_t[:, pl.ds(r, WIDE)] = mixed.T.astype(BF16)
    outs = Scatter(scatter_out, at)
    next(step)

    def multiply(sub, o, first=False):
        m = ring.ready(sub, o)
        cols = pl.ds(pl.multiple_of(m * 2 * WIDE, 2 * WIDE), 2 * WIDE)
        shards = jnp.concatenate([whole_out[2 * m], whole_out[2 * m + 1]], axis=1)
        part = lax.dot_general(
            upstream[:, cols], shards, (((1,), (1,)), ((), ())), preferred_element_type=F32
        )
        acc[...] = part if first else acc[...] + part

    loaded(4)
    multiply(0, 0, True)
    multiply(0, 1)
    multiply(0, -1)
    outs.partials(product_t, upstream, 0, 1)
    order = ((1, (0,)), (0, (2, -2)), (1, (1, -1)), (0, (3, -3)), (1, (2, -2)), (0, (4,)))
    for n, (sub, offsets) in enumerate(order):
        next(step)
        if n == 1:
            turn_out()
        for o in offsets:
            multiply(sub, o)
        if n < 5:
            outs.partials(product_t, upstream, n + 1, n + 2)
    multiply(1, 3)
    multiply(1, -3)
    for _ in step:
        pass
    multiply(1, 4)

    for r in range(0, ROWS, WIDE):
        rows = pl.ds(r, WIDE)
        conv = acc[rows, :] * outer_gate[rows, :].astype(F32)
        conv_t[:, rows] = conv.T.astype(BF16)
    exchange(lambda d: conv_t.at[sixteen(d)], conv_rx.at[sixteen(s)], conv_s, conv_r, s)
    conv_rx[sixteen(s), :] = conv_t[sixteen(s), :]

    @pl.when(away)
    def _():
        turn.wait_recv()

    @pl.when(jnp.logical_not(away))
    def _():
        stay.wait()

    ring_in = Gather(in_piece, whole_in, sems_in, at)
    ring_in.begin()
    in_step = ring_in.steps()
    for r in range(0, ROWS, WIDE):
        rows = pl.ds(r, WIDE)
        grad_outer[rows, :] = (acc[rows, :] * conv_output[rows, :].astype(F32)).astype(BF16)
    loaded(5, *range(7, 15))

    def filter_rows(j, _):
        other_f[sixteen(j), :] = filters[:, lanes_at(j)].astype(F32)
        return 0

    lax.fori_loop(0, OUTER, filter_rows, 0)
    spectra = Spectra(tables)

    def take_filter(i, _):
        spec_h[i] = spectra.forward(other_f, i)
        return 0

    lax.fori_loop(0, 4, take_filter, 0)
    next(in_step)
    lax.fori_loop(4, 8, take_filter, 0)
    outs.partials(product_t, upstream, 6, 8)
    out_step = outs.steps()
    next(out_step)
    next(in_step)

    arrived(lambda d: conv_rx.at[sixteen(d)], conv_s, conv_r, s)
    exchange(lambda d: mix_t.at[sixteen(d)], mix_rx.at[sixteen(s)], mix_s, mix_r, s)
    mix_rx[sixteen(s), :] = mix_t[sixteen(s), :]
    spread(conv_rx, conv_f)

    def take_mixed(i, _):
        spec = spectra.forward(conv_f, i)
        spec_g[i] = spec
        spectra.inverse(spec, spec_h[i], out_f, i)
        return 0

    lax.fori_loop(0, 3, take_mixed, 0)
    next(in_step)
    lax.fori_loop(3, 6, take_mixed, 0)
    next(in_step)
    lax.fori_loop(6, 8, take_mixed, 0)

    def gather_rows(n, _):
        for q in range(3):
            mixed_cols[sixteen(n), q * WIDE : (q + 1) * WIDE] = out_f[
                sixteen(3 * n + q), :
            ].astype(BF16)
        return 0

    lax.fori_loop(0, N_SEQ, gather_rows, 0)
    exchange(lambda d: mixed_cols.at[sixteen(d)], mixed_rx.at[sixteen(s)], back_s, back_r, s)
    mixed_rx[sixteen(s), :] = mixed_cols[sixteen(s), :]

    def take_long(i, _):
        spectra.inverse(spec_g[i], spectra.forward(other_f, i), out_f, i)
        return 0

    next(in_step)
    arrived(lambda d: mix_rx.at[sixteen(d)], mix_s, mix_r, s)
    spread(mix_rx, other_f)
    lax.fori_loop(0, 3, take_long, 0)
    next(in_step)
    lax.fori_loop(3, 6, take_long, 0)
    next(in_step)
    arrived(lambda d: mixed_rx.at[sixteen(d)], back_s, back_r, s)
    next(out_step)
    next(out_step)

    edge_back = remote(
        grads.at[pl.ds(0, 8)],
        halo_back,
        halo_sem.at[2],
        halo_sem.at[3],
        "seq",
        (s + N_SEQ - 1) % N_SEQ,
    )
    for r in range(0, ROWS, WIDE):
        rows = pl.ds(r, WIDE)
        mixed = mixed_rx[:, rows].astype(F32).T
        grads[rows, :] = mixed * gate[rows, :].astype(F32)
        if r == 0:
            edge_back.start()
        grad_inner[rows, :] = (mixed * smooth_rows(r)).astype(BF16)
    edge_back.wait_recv()
    grads[pl.ds(ROWS, 8), :] = jnp.where(s == N_SEQ - 1, 0.0, halo_back[...])
    for r in range(0, ROWS, WIDE):
        rows = pl.ds(r, WIDE)
        out = all_taps[pl.ds(0, 1), :] * grads[rows, :]
        for j in range(1, 3):
            out = out + all_taps[pl.ds(j, 1), :] * grads[pl.ds(r + j, WIDE), :]
        value[rows, :] = out.astype(BF16)
        value_t[:, rows] = out.T.astype(BF16)

    def block(sub, o):
        return (1 - low if sub else low) * 4 + (x + o + 4) % 4

    def x_hop(di, d, sub):
        o = -SIGNS[di] * (d - 1)
        return remote(
            value if (sub, o) == (0, 0) else blocks.at[block(sub, o)],
            blocks.at[block(sub, o)],
            x_s.at[di, d - 1, sub],
            x_r.at[di, d - 1, sub],
            "ch",
            low * 4 + (x + SIGNS[di] + 4) % 4,
        )

    def x_wait(di, d, sub):
        here = blocks.at[block(sub, -SIGNS[di] * d)]
        remote(
            here, here, x_s.at[di, d - 1, sub], x_r.at[di, d - 1, sub], "ch", ch
        ).wait_recv()

    partner = remote(
        value, blocks.at[block(0, 0)], p_s.at[0], p_s.at[1], "ch", (1 - low) * 4 + x
    )
    hops = []

    def x_go(di, d, sub):
        hop = x_hop(di, d, sub)
        hop.start()
        hops.append(hop)

    x_go(0, 1, 0)
    x_go(1, 1, 0)
    partner.start()
    next(out_step)
    blocks[block(0, 0)] = value[...]
    loaded(6)
    total = Scatter(scatter_in, at)
    total.partials(value_t, layer_input, 0, 3)
    step = total.steps()
    next(step)
    total.partials(value_t, layer_input, 3, 6)
    next(step)
    total.partials(value_t, layer_input, 6, 8)
    partner.wait_recv()
    x_go(0, 1, 1)
    x_go(1, 1, 1)
    x_wait(0, 1, 0)
    x_go(0, 2, 0)
    next(out_step)
    next(step)
    next(step)
    next(out_step)

    sums = []
    for j in range(3):
        part = jnp.zeros((1, CHANS), F32)
        for r in range(0, ROWS, WIDE):
            part = part + jnp.sum(
                grads[pl.ds(r, WIDE), :] * padded[pl.ds(8 + r - j, WIDE), :], axis=0, keepdims=True
            )
        sums.append(part)
    short_tx[...] = jnp.concatenate(sums + [jnp.zeros((5, CHANS), F32)], axis=0)
    exchange(lambda d: short_tx.at[:, lanes_at(d // 8)], short_rx.at[s], short_s, short_r, s)
    short_rx[s] = short_tx[:, lanes_at(s // 8)]

    x_wait(1, 1, 0)
    next(step)
    next(out_step)
    next(in_step)
    next(step)
    x_wait(1, 1, 1)
    x_go(1, 2, 1)
    next(out_step)
    next(in_step)
    next(step)
    for _ in out_step:
        pass
    for _ in in_step:
        pass
    lax.fori_loop(6, 8, take_long, 0)
    next(step)

    def long_rows(j, _):
        grad_long[:, lanes_at(j)] = out_f[sixteen(j), :]
        return 0

    lax.fori_loop(0, OUTER, long_rows, 0)
    for sub in range(2):
        for o in range(-3, 5):
            ring_in.ready(sub, o)

    def finish(n, first=False):
        w = jnp.concatenate([whole_in[4 * n + i] for i in range(4)], axis=0)
        part = lax.dot_general(
            blocks[n], w, (((1,), (1,)), ((), ())), preferred_element_type=F32
        )
        acc[...] = part if first else acc[...] + part

    finish(ch, True)
    finish(block(1, 0))
    finish(block(0, -1))
    finish(block(0, 1))
    finish(block(1, 1))
    for _ in step:
        pass
    outs.finish(grad_outproj)
    x_wait(0, 1, 1)
    finish(block(1, -1))
    total.finish(inproj_t)
    grad_inproj[...] = inproj_t[...].T
    arrived(lambda d: short_rx.at[d], short_s, short_r, s)
    tile = short_rx[0]
    for i in range(1, N_SEQ):
        tile = tile + short_rx[i]
    grad_short[...] = tile
    x_wait(0, 2, 0)
    finish(block(0, 2))
    x_wait(1, 2, 1)
    finish(block(1, 2))
    grad_input[...] = acc[...].astype(BF16)
    edge_back.wait_send()

    for hop in hops:
        hop.wait_send()
    partner.wait_send()
    edge.wait_send()
    ring.end()
    ring_in.end()

    @pl.when(away)
    def _():
        turn.wait_send()


    left(taps, taps_s, taps_r, s)
    left(mix_t.at[sixteen(0)], mix_s, mix_r, s)
    left(conv_t.at[sixteen(0)], conv_s, conv_r, s)
    left(mixed_cols.at[sixteen(0)], back_s, back_r, s)
    left(short_rx.at[0], short_s, short_r, s)


TAPS_AT = 4


def own_lanes():
    lane = (lax.axis_index("seq") % 8) * MINE
    rows = lax.broadcasted_iota(jnp.int32, (MINE, WIDE), 0)
    cols = lax.broadcasted_iota(jnp.int32, (MINE, WIDE), 1)
    return jnp.where(cols == rows + lane, 1.0, 0.0).astype(F32)


def hand_out(*refs):
    *refs, tile, sems = refs
    n = len(refs) // 3
    inward = [
        pltpu.make_async_copy(refs[i], tile if i == TAPS_AT else refs[2 * n + i], sems.at[i])
        for i in range(n)
    ]
    outward = [
        pltpu.make_async_copy(refs[2 * n + i], refs[n + i], sems.at[n + i]) for i in range(n)
    ]
    for copy in inward:
        copy.start()
    for i in range(n):
        inward[i].wait()
        if i != TAPS_AT:
            outward[i].start()
    refs[2 * n + TAPS_AT][...] = lax.dot_general(
        own_lanes(),
        tile[...],
        (((1,), (1,)), ((), ())),
        precision=lax.Precision.HIGHEST,
        preferred_element_type=F32,
    )[:, :3]
    outward[TAPS_AT].start()
    for copy in outward:
        copy.wait()


def shards(
    layer_input, value_proj, outer_gate, inner_gate, conv_output,
    upstream, in_weight, out_weight, long_filter, short_filter,
):
    dma = pltpu.SemaphoreType.DMA
    peers = dma((N_SEQ,))
    vmem = pltpu.VMEM
    tables = [jnp.asarray(t) for t in dft_tables()]
    outs = [
        jax.ShapeDtypeStruct(shape, dtype)
        for shape, dtype in (
            ((ROWS, CHANS), BF16),
            ((ROWS, CHANS), BF16),
            ((ROWS, CHANS), BF16),
            ((MINE, LENGTH), F32),
            ((8, WIDE), F32),
            ((WIDE, CHANS), F32),
            ((CHANS, WIDE), F32),
        )
    ]
    args = (
        layer_input, value_proj, outer_gate, inner_gate, conv_output, upstream, in_weight, out_weight,
        long_filter[0], short_filter[0], *tables,
    )
    local = [vmem((ROWS, CHANS), BF16)] * 4
    block = vmem((CHANS, ROWS), BF16)
    signal = vmem((MINE * OUTER, WIDE), F32)
    spectrum = vmem((MINE // 2, 2 * OUTER, 2 * WIDE), F32)
    scratch = [
        vmem((ROWS, DEEP), BF16),
        *local,
        vmem((ROWS, DEEP), BF16),
        vmem((MINE, LENGTH), BF16),
        *[vmem(t.shape, t.dtype) for t in tables],
        vmem((N_SEQ, CHANS, WIDE), BF16),
        vmem((N_SEQ, WIDE, CHANS), BF16),
        vmem((ROWS, CHANS), F32),
        *[block] * 7,
        vmem((ROWS, CHANS), BF16),
        block,
        vmem((8, ROWS, CHANS), BF16),
        vmem((ROWS + 8, CHANS), F32),
        vmem((8, CHANS), F32),
        vmem((16, CHANS), BF16),
        vmem((N_SEQ, 8, WIDE), F32),
        vmem((ROWS + 8, CHANS), F32),
        vmem((8, CHANS), F32),
        vmem((8, CHANS), F32),
        vmem((N_SEQ, 8, WIDE), F32),
        signal, signal, signal, spectrum, spectrum,
        vmem((WIDE, CHANS), BF16),
        vmem((CHANS, WIDE), F32),
        vmem((MINE, 3), F32), vmem((8, WIDE), F32),
        dma((16,)), dma((4,)), dma((3,)),
        *[peers] * 10,
        dma((2, 2, 2)), dma((2, 2, 2)), dma((2,)),
        *Gather.sems, *Gather.sems, *Scatter.scratch(), *Scatter.scratch(),
    ]
    given = list(outs)
    given[TAPS_AT] = jax.ShapeDtypeStruct((MINE, 3), F32)
    results = pl.pallas_call(
        whole_kernel,
        out_shape=outs,
        in_specs=[pl.BlockSpec(memory_space=pl.ANY)] * len(args),
        out_specs=[pl.BlockSpec(memory_space=pltpu.VMEM)] * len(outs),
        scratch_shapes=scratch,
        compiler_params=pltpu.CompilerParams(
            collective_id=0, has_side_effects=True, vmem_limit_bytes=60 * 2**20
        ),
        cost_estimate=pl.CostEstimate(
            flops=12 * 10**9, bytes_accessed=20 * 2**20, transcendentals=0
        ),
    )(*args)
    (
        grad_input, grad_outer, grad_inner, grad_long, grad_short, grad_inproj, grad_outproj,
    ) = pl.pallas_call(
        hand_out,
        out_shape=given,
        in_specs=[pl.BlockSpec(memory_space=pl.ANY)] * len(outs),
        out_specs=[pl.BlockSpec(memory_space=pl.ANY)] * len(outs),
        scratch_shapes=[
            *[vmem(o.shape, o.dtype) for o in given],
            vmem((8, WIDE), F32),
            dma((2 * len(outs),)),
        ],
    )(*results)
    return (
        grad_input,
        grad_outer,
        grad_inner,
        grad_long[None],
        grad_short[None],
        grad_inproj,
        grad_outproj,
    )


def solution(mesh):
    in_specs = (
        P("seq", None),
        P("seq", "ch"),
        P("seq", "ch"),
        P("seq", "ch"),
        P("seq", "ch"),
        P("seq", None),
        P("seq", "ch"),
        P("ch", "seq"),
        P("ch", "seq", None),
        P("ch", "seq", None),
    )
    out_specs = (
        P("seq", "ch"),
        P("seq", "ch"),
        P("seq", "ch"),
        P("ch", "seq", None),
        P("ch", "seq", None),
        P("seq", "ch"),
        P("ch", "seq"),
    )
    return jax.shard_map(shards, mesh=mesh, in_specs=in_specs, out_specs=out_specs, check_vma=False)
```
